32 devices in a mesh: lon: 2 (over y), mem: 16 (over z, x, core).
Axes of the slice: x: 2, y: 2, z: 4, core: 2. Of those that a mesh axis runs over, the one named last changes fastest.
Arguments:
- ensemble: float32 [16, 24576], P('mem', 'lon')
- increments: bfloat16 [16, 24576], P('mem', 'lon'), may hold values from -6 to 6
- offsets: int32 [48, 7], P('lon'), may hold values from -12 to 12, as said below
- taper: bfloat16 [8, 512, 512], replicated
Outputs:
- covariance_product: float32 [16, 24576], P('mem', 'lon')
The draws below stay inside these ranges and needn't reach their ends.
Inputs may be any that keep to these rules, and one draw needn't show every extreme that they name: Each row lists 7 different nonzero offsets in ascending order.
All inputs are finite; a program needn't handle non-finite values.
Results may differ from the reference program's by a relative error of at most 0.008.
Values may be sent and summed in bfloat16 or wider, within the bound.
No kernel may reach another device: no remote copies, remote signals or barrier semaphores. Data moves between devices by JAX's collectives and lax.ppermute only.
A program may use at most 64 MiB of HBM per device.

```python
import math
import jax
import jax.numpy as jnp
from jax import lax

BLOCK = 512
BLOCKS_DEV = 24
NEIGHBORS = 7
MEMBERS = 16
INCREMENTS = 16
NBLOCKS = 48
COLUMNS = 24576


def draw_ensemble(key, part):
    key_noise, key_column, key_background = jax.random.split(key, 3)
    member_index = jnp.arange(MEMBERS, dtype=jnp.float32)[:, None]
    member_scale = 0.5 * 3.2 ** (member_index / max(MEMBERS - 1, 1))
    column_scale = jnp.exp(jax.random.uniform(key_column, (1, COLUMNS), jnp.float32, math.log(0.5), math.log(1.5)))
    background = 24.0 * jax.random.normal(key_background, (1, COLUMNS), jnp.float32)
    spread = jnp.clip(jax.random.normal(key_noise, (MEMBERS, COLUMNS), jnp.float32), -5.0, 5.0)
    return (background + member_scale * column_scale * spread).astype(jnp.float32)


def draw_taper(key, part):
    fresh = jnp.clip(jax.random.normal(key, (NEIGHBORS + 1, BLOCK, BLOCK), jnp.float32), -5.0, 5.0)
    slot_index = jnp.arange(NEIGHBORS + 1)[:, None, None]
    identity = jnp.eye(BLOCK, dtype=jnp.float32)[None, :, :]
    tiles = jnp.where(slot_index == 0, identity + 0.4 / math.sqrt(BLOCK) * fresh, 0.5 / math.sqrt(BLOCK) * fresh)
    return tiles.astype(jnp.bfloat16)


def draw_offsets(key, part):
    reach_blocks = BLOCKS_DEV // 2
    choices_all = jnp.concatenate([jnp.arange(-reach_blocks, 0, dtype=jnp.int32), jnp.arange(1, reach_blocks + 1, dtype=jnp.int32)])
    width_all = 2 * reach_blocks
    row_keys = jax.random.split(key, NBLOCKS)
    position = jnp.arange(width_all, dtype=jnp.int32)
    extremes = (position == 0) | (position == width_all - 1)

    def single_row(row_key, row_number):
        shuffled = jax.random.permutation(row_key, width_all).astype(jnp.int32)
        ranking = jnp.argsort(shuffled).astype(jnp.int32)
        ranking = jnp.where((row_number == 0) & extremes, ranking - width_all, ranking)
        ordering = jnp.argsort(ranking)
        return jnp.sort(choices_all[ordering[:NEIGHBORS]])
    return jax.vmap(single_row)(row_keys, jnp.arange(NBLOCKS, dtype=jnp.int32)).astype(jnp.int32)


def shard_levels(stream_key, extent, pieces, least, top_value):
    loudness = 1.0
    for dim, parts in pieces:
        steps = jax.random.uniform(jax.random.fold_in(jax.random.fold_in(stream_key, 6), dim), (parts,), jnp.float32, least / len(pieces), top_value / len(pieces))
        loudness = loudness * jnp.repeat(jnp.exp(steps), extent[dim] // parts).reshape((-1,) + (1,) * (len(extent) - 1 - dim))
    return loudness


def normal_values(key, dims, scale, most, cuts=(), kind=jnp.bfloat16):
    result = jax.random.normal(key, dims, jnp.float32) * scale
    if len(cuts) > 0:
        result = shard_levels(key, dims, cuts, -0.22, 0.18) * result
    return jnp.clip(result, min=-most, max=most).astype(kind)


def setup_inputs(seed: int = 0) -> dict:
    key_of = jax.random.split(jax.random.key(seed), 5)
    ensemble = draw_ensemble(jax.random.fold_in(key_of[4], 71), 0)
    increments = normal_values(key_of[1], (INCREMENTS, COLUMNS), 1.0, 6.0, ((0, 16), (1, 2)))
    offsets = draw_offsets(jax.random.fold_in(key_of[4], 71), 0)
    taper = draw_taper(jax.random.fold_in(key_of[4], 71), 0)
    return {"ensemble": ensemble, "increments": increments, "offsets": offsets, "taper": taper}


def taper_apply(weighted, offsets, taper):
    vectors = weighted.shape[0]
    block_count = offsets.shape[0]
    blocks = weighted.reshape(vectors, block_count, BLOCK)
    block_rows = jnp.arange(block_count, dtype=jnp.int32)
    indices = jnp.concatenate([block_rows[:, None], (block_rows[:, None] + offsets) % block_count], axis=1).astype(jnp.int32)
    picked = jnp.take(blocks, indices, axis=1)
    tapered = jnp.einsum("qrsb,sab->qra", picked.astype(jnp.float32), taper.astype(jnp.float32))
    return tapered.reshape(vectors, block_count * BLOCK)


def reference(ensemble, increments, offsets, taper):
    ens_mean = jnp.sum(ensemble, axis=0) / MEMBERS
    perturb = (ensemble - ens_mean[None, :]).astype(jnp.bfloat16)

    def accumulate(member, summed):
        member_row = lax.dynamic_index_in_dim(perturb, member, 0, keepdims=False).astype(jnp.float32)
        weighted = (member_row[None, :] * increments.astype(jnp.float32)).astype(jnp.bfloat16)
        tapered = taper_apply(weighted, offsets, taper)
        return summed + member_row[None, :] * tapered

    summed = lax.fori_loop(0, MEMBERS, accumulate, jnp.zeros((INCREMENTS, COLUMNS), jnp.float32))
    return summed / (MEMBERS - 1)
```

```python
import functools

import jax
import jax.numpy as jnp
from jax import lax
from jax.experimental import pallas as pl
from jax.experimental.pallas import tpu as pltpu
from jax.sharding import PartitionSpec as P

LANES = 128
SUB = 8


def product_kernel(
    group, off_ref, *refs
):
    own, other = refs[:4], refs[4:8]
    inc_own, inc_other, taper_hbm, out_ref = refs[8:12]
    tiles, pert, wide, picked_from, picked, acc, sems = refs[12:]
    slots, block_size, _ = tiles.shape
    members = 4 * group
    rows = inc_own.shape[0]
    quarters = block_size // LANES
    block_count = rows // quarters
    copies = []
    for s in range(slots):
        copies.append(pltpu.make_async_copy(taper_hbm.at[s], tiles.at[s], sems.at[s]))
        copies[-1].start()

    def weigh(side, groups, inc_ref, keep):
        def chunk(r, carry):
            at = pl.multiple_of(r * 2 * SUB, 2 * SUB)
            inc = inc_ref[pl.ds(at, 2 * SUB), :].astype(jnp.float32)
            states = [
                groups[g][j, pl.ds(at, 2 * SUB), :]
                for g in range(4)
                for j in range(group)
            ]
            total = states[0]
            for state in states[1:]:
                total = total + state
            mean = total * (1.0 / members)
            for m, state in enumerate(states):
                p = (state - mean).astype(jnp.bfloat16).astype(jnp.float32)
                if keep:
                    pert[pl.ds(m * rows + at, 2 * SUB), :] = p
                wide[pl.ds(m * rows + at, 2 * SUB), :] = p * inc
            return carry

        lax.fori_loop(0, rows // (2 * SUB), chunk, 0)

        def spread(i, carry):
            for q in range(quarters):
                part = wide[pl.ds(i * quarters + q, members, rows), :]
                picked_from[side * block_count + i, :, q * LANES : (q + 1) * LANES] = (
                    part.astype(jnp.bfloat16)
                )
            return carry

        lax.fori_loop(0, block_count, spread, 0, unroll=4)

    weigh(1, other, inc_other, False)
    weigh(0, own, inc_own, True)

    contract = (((1,), (1,)), ((), ()))
    copies[0].wait()
    vectors = block_count * members
    acc[...] = lax.dot_general(
        picked_from[0:block_count].reshape(vectors, block_size),
        tiles[0],
        contract,
        preferred_element_type=jnp.float32,
    )
    for s in range(1, slots):
        for i in range(block_count):
            place = i + off_ref[s - 1, i]
            place = jnp.where(place < 0, place + 2 * block_count, place)
            picked[i * members : (i + 1) * members, :] = picked_from[place]
        copies[s].wait()
        acc[...] += lax.dot_general(
            picked[...], tiles[s], contract, preferred_element_type=jnp.float32
        )

    scale = 1.0 / (members - 1)
    for i in range(block_count):
        for q in range(quarters):
            lanes = slice(q * LANES, (q + 1) * LANES)
            term = (
                pert[pl.ds(i * quarters + q, members, rows), :]
                * acc[i * members : (i + 1) * members, lanes]
            )
            row = jnp.sum(term, axis=0, keepdims=True) * scale
            out_ref[:, i * block_size + q * LANES : i * block_size + (q + 1) * LANES] = row


def mover(lon_size, mem_size):
    def one(x, step, mem_of):
        perm = []
        for l in range(lon_size):
            for m in range(mem_size):
                source = ((l + step) % lon_size) * mem_size + mem_of(m)
                perm.append((source, l * mem_size + m))
        return lax.ppermute(x, ("lon", "mem"), perm)

    def move(x, across, mem_of):
        if not across:
            return one(x, 0, mem_of)
        if lon_size == 2:
            return one(x, 1, mem_of)
        half = x.shape[-2] // 2
        right = one(x[..., :half, :], 1, mem_of)
        left = one(x[..., half:, :], -1, mem_of)
        return jnp.concatenate([right, left], axis=-2)

    return move


def on_device(ensemble, increments, offsets, taper):
    lon_size, mem_size = lax.axis_size("lon"), lax.axis_size("mem")
    group = mem_size // 4
    slots, block_size, _ = taper.shape
    block_count = offsets.shape[0]
    columns = ensemble.shape[1]
    rows = columns // LANES
    move = mover(lon_size, mem_size)

    state = ensemble.reshape(1, rows, LANES)
    inc = increments.reshape(rows, LANES)
    inc_other = move(inc, True, lambda m: m)
    states = [state]
    for d in range(1, group):
        states.append(move(state, False, lambda m: (m + 4 * d) % mem_size))
    mine = jnp.concatenate(states, axis=0)
    groups = [
        mine,
        move(mine, False, lambda m: m ^ 2),
        move(mine, True, lambda m: m),
        move(mine, True, lambda m: m ^ 2),
    ]
    groups += [move(g, False, lambda m: m ^ 1) for g in groups]
    own = [groups[i] for i in (0, 1, 4, 5)]
    other = [groups[i] for i in (2, 3, 6, 7)]

    vectors = mem_size * block_count
    whole = pl.BlockSpec(memory_space=pltpu.VMEM)
    return pl.pallas_call(
        functools.partial(product_kernel, group),
        out_shape=jax.ShapeDtypeStruct((1, columns), jnp.float32),
        in_specs=[pl.BlockSpec(memory_space=pltpu.SMEM)]
        + [whole] * 10
        + [pl.BlockSpec(memory_space=pl.ANY)],
        out_specs=whole,
        scratch_shapes=[
            pltpu.VMEM((slots, block_size, block_size), jnp.bfloat16),
            pltpu.VMEM((mem_size * rows, LANES), jnp.float32),
            pltpu.VMEM((mem_size * rows, LANES), jnp.float32),
            pltpu.VMEM((2 * block_count, mem_size, block_size), jnp.bfloat16),
            pltpu.VMEM((vectors, block_size), jnp.bfloat16),
            pltpu.VMEM((vectors, block_size), jnp.float32),
            pltpu.SemaphoreType.DMA((slots,)),
        ],
        compiler_params=pltpu.CompilerParams(vmem_limit_bytes=48 * 1024 * 1024),
    )(offsets.T, *own, *other, inc, inc_other, taper)


def solution(mesh):
    return jax.shard_map(
        on_device,
        mesh=mesh,
        in_specs=(P("mem", "lon"), P("mem", "lon"), P("lon", None), P()),
        out_specs=P("mem", "lon"),
        check_vma=False,
    )
```

```python
import functools

import jax
import jax.numpy as jnp
from jax import lax
from jax.experimental import pallas as pl
from jax.experimental.pallas import tpu as pltpu
from jax.sharding import PartitionSpec as P

LANES = 128
SUB = 8
VMEM_LIMIT = 51 * 1024 * 1024


def product_kernel(group, places, *refs):
    own, other = refs[:4], refs[4:8]
    inc_own, inc_other, taper_hbm, out_ref = refs[8:12]
    tiles, pert, picked_from, picked, acc, sems = refs[12:]
    slots, block_size, _ = tiles.shape
    members = 4 * group
    rows = own[0].shape[1]
    pitch = pert.shape[0] // members
    quarters = block_size // LANES
    block_count = rows // quarters
    copies = []
    for s in range(slots):
        copies.append(pltpu.make_async_copy(taper_hbm.at[s], tiles.at[s], sems.at[s]))
        copies[-1].start()

    def weigh(side, groups, inc_ref):
        def chunk(r, carry):
            at = pl.multiple_of(r * SUB, SUB)
            states = [
                groups[g][j, pl.ds(at, SUB), :] for g in range(4) for j in range(group)
            ]
            total = states[0]
            for state in states[1:]:
                total = total + state
            mean = total * (1.0 / members)
            for m, state in enumerate(states):
                pert[pl.ds(m * pitch + at, SUB), :] = (
                    (state - mean).astype(jnp.bfloat16).astype(jnp.float32)
                )
            return carry

        lax.fori_loop(0, rows // SUB, chunk, 0, unroll=2)

        for i in range(block_count):
            for q in range(quarters):
                lanes = slice(q * LANES, (q + 1) * LANES)
                at = i * quarters + q
                inc = inc_ref[:, at * LANES : (at + 1) * LANES].astype(jnp.float32)
                part = pert[pl.ds(at, members, pitch), :] * inc
                picked_from[side * block_count + i, :, lanes] = part.astype(jnp.bfloat16)

    weigh(1, other, inc_other)
    weigh(0, own, inc_own)

    contract = (((1,), (1,)), ((), ()))
    copies[0].wait()
    vectors = block_count * members
    acc[...] = lax.dot_general(
        picked_from[0:block_count].reshape(vectors, block_size),
        tiles[0],
        contract,
        preferred_element_type=jnp.float32,
    )
    for s in range(1, slots):
        for i in range(block_count):
            rows_of = slice(i * members, (i + 1) * members)
            picked[s - 1, rows_of, :] = picked_from[places[s - 1, i]]
        copies[s].wait()
        acc[...] += lax.dot_general(
            picked[s - 1], tiles[s], contract, preferred_element_type=jnp.float32
        )

    scale = 1.0 / (members - 1)
    for i in range(block_count):
        for q in range(quarters):
            lanes = slice(q * LANES, (q + 1) * LANES)
            term = (
                pert[pl.ds(i * quarters + q, members, pitch), :]
                * acc[i * members : (i + 1) * members, lanes]
            )
            row = jnp.sum(term, axis=0, keepdims=True) * scale
            out_ref[:, i * block_size + q * LANES : i * block_size + (q + 1) * LANES] = row


def mover(lon_size, mem_size):
    def one(x, step, mem_of):
        perm = []
        for l in range(lon_size):
            for m in range(mem_size):
                source = ((l + step) % lon_size) * mem_size + mem_of(m)
                perm.append((source, l * mem_size + m))
        return lax.ppermute(x, ("lon", "mem"), perm)

    def move(x, across, mem_of):
        if not across:
            return one(x, 0, mem_of)
        if lon_size == 2:
            return one(x, 1, mem_of)
        axis = x.ndim - 2 if x.shape[-2] > 1 else x.ndim - 1
        right, left = jnp.split(x, 2, axis=axis)
        return jnp.concatenate([one(right, 1, mem_of), one(left, -1, mem_of)], axis=axis)

    return move


def on_device(ensemble, increments, offsets, taper):
    lon_size, mem_size = lax.axis_size("lon"), lax.axis_size("mem")
    group = mem_size // 4
    slots, block_size, _ = taper.shape
    block_count = offsets.shape[0]
    columns = ensemble.shape[1]
    rows = columns // LANES
    move = mover(lon_size, mem_size)

    state = ensemble.reshape(rows, LANES)
    inc_other = move(increments.reshape(1, columns), True, lambda m: m)
    lines = [[j + 4 * i for i in range(group)] for j in range(4)]
    sent = jnp.broadcast_to(state, (group, rows, LANES))
    mine = lax.all_to_all(sent, "mem", 0, 0, axis_index_groups=lines, tiled=True)
    inc_own = increments.astype(jnp.float32)
    places = jnp.arange(block_count, dtype=jnp.int32) + offsets.T
    places = jnp.where(places < 0, places + 2 * block_count, places)
    mine, inc_other, inc_own, places = lax.optimization_barrier(
        (mine, inc_other, inc_own, places)
    )
    groups = [
        mine,
        move(mine, False, lambda m: m ^ 2),
        move(mine, True, lambda m: m),
        move(mine, True, lambda m: m ^ 2),
    ]
    groups += [move(g, False, lambda m: m ^ 1) for g in groups]
    own = [groups[i] for i in (0, 1, 4, 5)]
    other = [groups[i] for i in (2, 3, 6, 7)]

    vectors = mem_size * block_count
    whole = pl.BlockSpec(memory_space=pltpu.VMEM)
    return pl.pallas_call(
        functools.partial(product_kernel, group),
        out_shape=jax.ShapeDtypeStruct((1, columns), jnp.float32),
        in_specs=[pl.BlockSpec(memory_space=pltpu.SMEM)]
        + [whole] * 10
        + [pl.BlockSpec(memory_space=pltpu.HBM)],
        out_specs=whole,
        scratch_shapes=[
            pltpu.VMEM((slots, block_size, block_size), jnp.bfloat16),
            pltpu.VMEM((mem_size * (rows + 1), LANES), jnp.float32),
            pltpu.VMEM((2 * block_count, mem_size, block_size), jnp.bfloat16),
            pltpu.VMEM((slots - 1, vectors, block_size), jnp.bfloat16),
            pltpu.VMEM((vectors, block_size), jnp.float32),
            pltpu.SemaphoreType.DMA((slots,)),
        ],
        compiler_params=pltpu.CompilerParams(vmem_limit_bytes=VMEM_LIMIT),
    )(places, *own, *other, inc_own, inc_other, taper)


def solution(mesh):
    return jax.shard_map(
        on_device,
        mesh=mesh,
        in_specs=(P("mem", "lon"), P("mem", "lon"), P("lon", None), P()),
        out_specs=P("mem", "lon"),
        check_vma=False,
    )
```

```python
import functools

import jax
import jax.numpy as jnp
from jax import lax
from jax.experimental import pallas as pl
from jax.experimental.pallas import tpu as pltpu
from jax.sharding import PartitionSpec as P

LANES = 128
SUB = 8
VMEM_LIMIT = 51 * 1024 * 1024


def product_kernel(group, places, *refs):
    own, other = (refs[:4], refs[4:8]), (refs[8:12], refs[12:16])
    inc_own, inc_other, taper_hbm, out_ref = refs[16:20]
    tiles, pert, picked_from, picked, acc, sems = refs[20:]
    slots, block_size, _ = tiles.shape
    members = 4 * group
    rows = own[0][0].shape[0]
    pitch = pert.shape[0] // members
    quarters = block_size // LANES
    block_count = rows // quarters
    copies = []
    for s in range(slots):
        copies.append(pltpu.make_async_copy(taper_hbm.at[s], tiles.at[s], sems.at[s]))
        copies[-1].start()

    def weigh(side, bases, diffs, inc_ref):
        def chunk(r, carry):
            at = pl.multiple_of(r * 2 * SUB, 2 * SUB)
            starts = [ref[pl.ds(at, 2 * SUB), :] for ref in bases]
            steps = [
                [ref[j, pl.ds(at, 2 * SUB), :].astype(jnp.float32) for j in range(group - 1)]
                for ref in diffs
            ]
            total = sum(step for line in steps for step in line) + group * sum(starts)
            mean = total * (1.0 / members)
            m = 0
            for start, line in zip(starts, steps):
                start = start - mean
                for value in [start] + [start + step for step in line]:
                    pert[pl.ds(m * pitch + at, 2 * SUB), :] = value
                    m += 1
            return carry

        lax.fori_loop(0, rows // (2 * SUB), chunk, 0, unroll=2)

        for i in range(block_count):
            for q in range(quarters):
                lanes = slice(q * LANES, (q + 1) * LANES)
                at = i * quarters + q
                inc = inc_ref[:, at * LANES : (at + 1) * LANES].astype(jnp.float32)
                part = pert[pl.ds(at, members, pitch), :] * inc
                picked_from[side * block_count + i, :, lanes] = part.astype(jnp.bfloat16)

    weigh(1, *other, inc_other)
    weigh(0, *own, inc_own)

    contract = (((1,), (1,)), ((), ()))
    copies[0].wait()
    vectors = block_count * members
    acc[...] = lax.dot_general(
        picked_from[0:block_count].reshape(vectors, block_size),
        tiles[0],
        contract,
        preferred_element_type=jnp.float32,
    )
    for s in range(1, slots):
        for i in range(block_count):
            rows_of = slice(i * members, (i + 1) * members)
            picked[s - 1, rows_of, :] = picked_from[places[s - 1, i]]
        copies[s].wait()
        acc[...] += lax.dot_general(
            picked[s - 1], tiles[s], contract, preferred_element_type=jnp.float32
        )

    scale = 1.0 / (members - 1)
    for i in range(block_count):
        for q in range(quarters):
            lanes = slice(q * LANES, (q + 1) * LANES)
            term = (
                pert[pl.ds(i * quarters + q, members, pitch), :]
                * acc[i * members : (i + 1) * members, lanes]
            )
            row = jnp.sum(term, axis=0, keepdims=True) * scale
            out_ref[:, i * block_size + q * LANES : i * block_size + (q + 1) * LANES] = row


def mover(lon_size, mem_size):
    def one(x, step, mem_of):
        perm = []
        for l in range(lon_size):
            for m in range(mem_size):
                source = ((l + step) % lon_size) * mem_size + mem_of(m)
                perm.append((source, l * mem_size + m))
        return lax.ppermute(x, ("lon", "mem"), perm)

    def move(x, across, mem_of):
        if not across:
            return one(x, 0, mem_of)
        if lon_size == 2:
            return one(x, 1, mem_of)
        axis = x.ndim - 2 if x.shape[-2] > 1 else x.ndim - 1
        right, left = jnp.split(x, 2, axis=axis)
        return jnp.concatenate([one(right, 1, mem_of), one(left, -1, mem_of)], axis=axis)

    return move


def on_device(ensemble, increments, offsets, taper):
    lon_size, mem_size = lax.axis_size("lon"), lax.axis_size("mem")
    group = mem_size // 4
    slots, block_size, _ = taper.shape
    block_count = offsets.shape[0]
    columns = ensemble.shape[1]
    rows = columns // LANES
    move = mover(lon_size, mem_size)
    same, beside = (lambda m: m), (lambda m: m ^ 2)

    base = ensemble.reshape(rows, LANES)
    inc_other = move(increments.reshape(1, columns), True, same)
    partner = move(base, False, lambda m: m ^ 1)
    bases = [
        move(base, False, beside),
        move(base, True, same),
        move(base, True, beside),
    ]
    line = [
        move(base, False, lambda m: (m + 4 * d) % mem_size) for d in reversed(range(1, group))
    ]
    inc_own = increments.astype(jnp.float32)
    places = jnp.arange(block_count, dtype=jnp.int32) + offsets.T
    places = jnp.where(places < 0, places + 2 * block_count, places)
    line, bases, partner, inc_other, inc_own, places = lax.optimization_barrier(
        (line, bases, partner, inc_other, inc_own, places)
    )

    diff = (jnp.stack(line) - base[None]).astype(jnp.bfloat16)
    base = jnp.where(places[0, 0] < 2 * block_count, base, 0.0)
    diffs = [
        diff,
        move(diff, False, beside),
        move(diff, True, same),
        move(diff, True, beside),
    ]
    bases = [base] + bases + [partner] + [move(x, False, lambda m: m ^ 1) for x in bases]
    diffs += [move(x, False, lambda m: m ^ 1) for x in diffs]
    own, other = (0, 1, 4, 5), (2, 3, 6, 7)
    operands = [arrays[i] for side in (own, other) for arrays in (bases, diffs) for i in side]

    vectors = mem_size * block_count
    whole = pl.BlockSpec(memory_space=pltpu.VMEM)
    return pl.pallas_call(
        functools.partial(product_kernel, group),
        out_shape=jax.ShapeDtypeStruct((1, columns), jnp.float32),
        in_specs=[pl.BlockSpec(memory_space=pltpu.SMEM)]
        + [whole] * 18
        + [pl.BlockSpec(memory_space=pltpu.HBM)],
        out_specs=whole,
        scratch_shapes=[
            pltpu.VMEM((slots, block_size, block_size), jnp.bfloat16),
            pltpu.VMEM((mem_size * (rows + 1), LANES), jnp.float32),
            pltpu.VMEM((2 * block_count, mem_size, block_size), jnp.bfloat16),
            pltpu.VMEM((slots - 1, vectors, block_size), jnp.bfloat16),
            pltpu.VMEM((vectors, block_size), jnp.float32),
            pltpu.SemaphoreType.DMA((slots,)),
        ],
        compiler_params=pltpu.CompilerParams(vmem_limit_bytes=VMEM_LIMIT),
    )(places, *operands, inc_own, inc_other, taper)


def solution(mesh):
    return jax.shard_map(
        on_device,
        mesh=mesh,
        in_specs=(P("mem", "lon"), P("mem", "lon"), P("lon", None), P()),
        out_specs=P("mem", "lon"),
        check_vma=False,
    )
```

```python
import functools

import jax
import jax.numpy as jnp
from jax import lax
from jax.experimental import pallas as pl
from jax.experimental.pallas import tpu as pltpu
from jax.sharding import PartitionSpec as P

LANES = 128
SUB = 8
VMEM_LIMIT = 51 * 1024 * 1024


def split_kernel(base_ref, inc_ref, split_ref, wide_ref):
    base = base_ref[...]
    high = base.astype(jnp.bfloat16)
    rest = base - high.astype(jnp.float32)
    middle = rest.astype(jnp.bfloat16)
    split_ref[0] = high
    split_ref[1] = middle
    split_ref[2] = (rest - middle.astype(jnp.float32)).astype(jnp.bfloat16)
    wide_ref[...] = inc_ref[...].astype(jnp.float32)


def pack_kernel(split_ref, *refs):
    line, out_ref = refs[:-1], refs[-1]
    high, middle, low = (split_ref[i].astype(jnp.float32) for i in range(3))
    base = high + middle + low
    out_ref[0:3] = split_ref[...]
    for j, ref in enumerate(line):
        out_ref[3 + j] = (ref[...] - base).astype(jnp.bfloat16)


def product_kernel(group, places, *refs):
    own, other = refs[:4], refs[4:8]
    inc_own, inc_other, taper_hbm, out_ref = refs[8:12]
    tiles, pert, picked_from, picked, acc, sems = refs[12:]
    slots, block_size, _ = taper_hbm.shape
    members = 4 * group
    rows = own[0].shape[1]
    pitch = pert.shape[0] // members
    quarters = block_size // LANES
    block_count = rows // quarters
    copies = []
    for s in range(slots):
        depth = slice(s * block_size, (s + 1) * block_size)
        copies.append(pltpu.make_async_copy(taper_hbm.at[s], tiles.at[:, depth], sems.at[s]))
        copies[-1].start()

    def weigh(side, groups, inc_ref):
        def chunk(r, carry):
            at = pl.multiple_of(r * 2 * SUB, 2 * SUB)
            starts, steps = [], []
            for ref in groups:
                parts = [
                    ref[j, pl.ds(at, 2 * SUB), :].astype(jnp.float32) for j in range(group + 2)
                ]
                starts.append(parts[0] + parts[1] + parts[2])
                steps.append(parts[3:])
            total = sum(step for line in steps for step in line) + group * sum(starts)
            mean = total * (1.0 / members)
            m = 0
            for start, line in zip(starts, steps):
                start = start - mean
                for value in [start] + [start + step for step in line]:
                    pert[pl.ds(m * pitch + at, 2 * SUB), :] = value
                    m += 1
            return carry

        lax.fori_loop(0, rows // (2 * SUB), chunk, 0, unroll=2)

        for i in range(block_count):
            for q in range(quarters):
                lanes = slice(q * LANES, (q + 1) * LANES)
                at = i * quarters + q
                inc = inc_ref[:, at * LANES : (at + 1) * LANES].astype(jnp.float32)
                part = pert[pl.ds(at, members, pitch), :] * inc
                picked_from[side * block_count + i, :, lanes] = part.astype(jnp.bfloat16)

    weigh(1, other, inc_other)
    weigh(0, own, inc_own)

    for i in range(block_count):
        rows_of = slice(i * members, (i + 1) * members)
        picked[rows_of, 0:block_size] = picked_from[i]
        for s in range(1, slots):
            depth = slice(s * block_size, (s + 1) * block_size)
            picked[rows_of, depth] = picked_from[places[s - 1, i]]
    for copy in copies:
        copy.wait()
    acc[...] = lax.dot_general(
        picked[...], tiles[...], (((1,), (1,)), ((), ())), preferred_element_type=jnp.float32
    )

    scale = 1.0 / (members - 1)
    for i in range(block_count):
        for q in range(quarters):
            lanes = slice(q * LANES, (q + 1) * LANES)
            term = (
                pert[pl.ds(i * quarters + q, members, pitch), :]
                * acc[i * members : (i + 1) * members, lanes]
            )
            row = jnp.sum(term, axis=0, keepdims=True) * scale
            out_ref[:, i * block_size + q * LANES : i * block_size + (q + 1) * LANES] = row


def mover(lon_size, mem_size):
    def one(x, step, mem_of):
        perm = []
        for l in range(lon_size):
            for m in range(mem_size):
                source = ((l + step) % lon_size) * mem_size + mem_of(m)
                perm.append((source, l * mem_size + m))
        return lax.ppermute(x, ("lon", "mem"), perm)

    def move(x, across, mem_of):
        if not across:
            return one(x, 0, mem_of)
        if lon_size == 2:
            return one(x, 1, mem_of)
        axis = x.ndim - 2 if x.shape[-2] > 1 else x.ndim - 1
        right, left = jnp.split(x, 2, axis=axis)
        return jnp.concatenate([one(right, 1, mem_of), one(left, -1, mem_of)], axis=axis)

    return move


def on_device(ensemble, increments, offsets, taper):
    lon_size, mem_size = lax.axis_size("lon"), lax.axis_size("mem")
    group = mem_size // 4
    slots, block_size, _ = taper.shape
    block_count = offsets.shape[0]
    columns = ensemble.shape[1]
    rows = columns // LANES
    move = mover(lon_size, mem_size)
    same, beside = (lambda m: m), (lambda m: m ^ 2)

    base = ensemble.reshape(rows, LANES)
    line = [
        move(base, False, lambda m: (m + 4 * d) % mem_size) for d in reversed(range(1, group))
    ]
    inc_other = move(increments.reshape(1, columns), True, same)
    places = jnp.arange(block_count, dtype=jnp.int32) + offsets.T
    places = jnp.where(places < 0, places + 2 * block_count, places)
    whole = pl.BlockSpec(memory_space=pltpu.VMEM)
    split, inc_own = pl.pallas_call(
        split_kernel,
        out_shape=(
            jax.ShapeDtypeStruct((3, rows, LANES), jnp.bfloat16),
            jax.ShapeDtypeStruct((1, columns), jnp.float32),
        ),
        in_specs=[whole] * 2,
        out_specs=(whole, whole),
    )(base, increments)
    split, inc_own, places, inc_other, line = lax.optimization_barrier(
        (split, inc_own, places, inc_other, line)
    )

    mine = pl.pallas_call(
        pack_kernel,
        out_shape=jax.ShapeDtypeStruct((group + 2, rows, LANES), jnp.bfloat16),
        in_specs=[whole] * group,
        out_specs=whole,
    )(split, *line)
    groups = [
        mine,
        move(mine, False, beside),
        move(mine, True, same),
        move(mine, True, beside),
    ]
    groups += [move(x, False, lambda m: m ^ 1) for x in groups]
    operands = [groups[i] for i in (0, 1, 4, 5, 2, 3, 6, 7)]

    vectors = mem_size * block_count
    return pl.pallas_call(
        functools.partial(product_kernel, group),
        out_shape=jax.ShapeDtypeStruct((1, columns), jnp.float32),
        in_specs=[pl.BlockSpec(memory_space=pltpu.SMEM)]
        + [whole] * 10
        + [pl.BlockSpec(memory_space=pltpu.HBM)],
        out_specs=whole,
        scratch_shapes=[
            pltpu.VMEM((block_size, slots * block_size), jnp.bfloat16),
            pltpu.VMEM((mem_size * (rows + 1), LANES), jnp.float32),
            pltpu.VMEM((2 * block_count, mem_size, block_size), jnp.bfloat16),
            pltpu.VMEM((vectors, slots * block_size), jnp.bfloat16),
            pltpu.VMEM((vectors, block_size), jnp.float32),
            pltpu.SemaphoreType.DMA((slots,)),
        ],
        compiler_params=pltpu.CompilerParams(vmem_limit_bytes=VMEM_LIMIT),
    )(places, *operands, inc_own, inc_other, taper)


def solution(mesh):
    return jax.shard_map(
        on_device,
        mesh=mesh,
        in_specs=(P("mem", "lon"), P("mem", "lon"), P("lon", None), P()),
        out_specs=P("mem", "lon"),
        check_vma=False,
    )
```

```python
import functools

import jax
import jax.numpy as jnp
from jax import lax
from jax.experimental import pallas as pl
from jax.experimental.pallas import tpu as pltpu
from jax.sharding import PartitionSpec as P

LANES = 128
SUB = 8
VMEM_LIMIT = 51 * 1024 * 1024
PACK_COST = 20_000_000_000


def pack_kernel(*refs):
    diff_ref, bases_ref = refs[-2:]
    bases, line = refs[:4], refs[4:-2]
    base = bases[0][...]
    for j, ref in enumerate(line):
        diff_ref[j] = (ref[...] - base).astype(jnp.bfloat16)
    for j, ref in enumerate(bases):
        bases_ref[j] = ref[...]


def product_kernel(group, off_ref, *refs):
    bases, diffs = refs[:2], refs[2:10]
    inc_own, inc_other, taper_hbm, out_ref = refs[10:14]
    tiles, pert, picked_from, picked, acc, sems = refs[14:]
    slots, block_size, _ = tiles.shape
    members = 4 * group
    rows = bases[0].shape[1]
    pitch = pert.shape[0] // members
    quarters = block_size // LANES
    block_count = rows // quarters
    copies = []
    for s in range(slots):
        copies.append(pltpu.make_async_copy(taper_hbm.at[s], tiles.at[s], sems.at[s]))
        copies[-1].start()

    def weigh(side, inc_ref):
        lines = [(c, 2 * side + j) for c in range(2) for j in range(2)]

        def chunk(r, carry):
            at = pl.multiple_of(r * 2 * SUB, 2 * SUB)
            here = pl.ds(at, 2 * SUB)
            starts = [bases[c][j, here, :] for c, j in lines]
            steps = [
                [diffs[4 * c + j][k, here, :].astype(jnp.float32) for k in range(group - 1)]
                for c, j in lines
            ]
            total = sum(step for line in steps for step in line) + group * sum(starts)
            mean = total * (1.0 / members)
            m = 0
            for start, line in zip(starts, steps):
                start = start - mean
                for value in [start] + [start + step for step in line]:
                    pert[pl.ds(m * pitch + at, 2 * SUB), :] = value
                    m += 1
            return carry

        lax.fori_loop(0, rows // (2 * SUB), chunk, 0, unroll=2)

        for i in range(block_count):
            for q in range(quarters):
                lanes = slice(q * LANES, (q + 1) * LANES)
                at = i * quarters + q
                inc = inc_ref[:, at * LANES : (at + 1) * LANES].astype(jnp.float32)
                part = pert[pl.ds(at, members, pitch), :] * inc
                picked_from[side * block_count + i, :, lanes] = part.astype(jnp.bfloat16)

    weigh(1, inc_other)
    weigh(0, inc_own)

    contract = (((1,), (1,)), ((), ()))
    vectors = block_count * members
    copies[0].wait()
    acc[...] = lax.dot_general(
        picked_from[0:block_count].reshape(vectors, block_size),
        tiles[0],
        contract,
        preferred_element_type=jnp.float32,
    )
    for s in range(1, slots):
        for i in range(block_count):
            rows_of = slice(i * members, (i + 1) * members)
            place = i + off_ref[s - 1, i]
            place = jnp.where(place < 0, place + 2 * block_count, place)
            picked[s - 1, rows_of, :] = picked_from[place]
        copies[s].wait()
        acc[...] += lax.dot_general(
            picked[s - 1], tiles[s], contract, preferred_element_type=jnp.float32
        )

    scale = 1.0 / (members - 1)
    for i in range(block_count):
        for q in range(quarters):
            lanes = slice(q * LANES, (q + 1) * LANES)
            term = (
                pert[pl.ds(i * quarters + q, members, pitch), :]
                * acc[i * members : (i + 1) * members, lanes]
            )
            row = jnp.sum(term, axis=0, keepdims=True) * scale
            out_ref[:, i * block_size + q * LANES : i * block_size + (q + 1) * LANES] = row


def mover(lon_size, mem_size):
    def one(x, step, mem_of):
        perm = []
        for l in range(lon_size):
            for m in range(mem_size):
                source = ((l + step) % lon_size) * mem_size + mem_of(m)
                perm.append((source, l * mem_size + m))
        return lax.ppermute(x, ("lon", "mem"), perm)

    def move(x, across, mem_of):
        if not across:
            return one(x, 0, mem_of)
        if lon_size == 2:
            return one(x, 1, mem_of)
        axis = x.ndim - 2 if x.shape[-2] > 1 else x.ndim - 1
        right, left = jnp.split(x, 2, axis=axis)
        return jnp.concatenate([one(right, 1, mem_of), one(left, -1, mem_of)], axis=axis)

    return move


def on_device(ensemble, increments, offsets, taper):
    lon_size, mem_size = lax.axis_size("lon"), lax.axis_size("mem")
    group = mem_size // 4
    slots, block_size, _ = taper.shape
    block_count = offsets.shape[0]
    columns = ensemble.shape[1]
    rows = columns // LANES
    move = mover(lon_size, mem_size)
    same, beside = (lambda m: m), (lambda m: m ^ 2)

    base = ensemble.reshape(rows, LANES)
    line = [
        move(base, False, lambda m: (m + 4 * d) % mem_size) for d in reversed(range(1, group))
    ]
    around = [
        move(base, False, beside),
        move(base, True, same),
        move(base, True, beside),
    ]
    inc_other = move(increments.reshape(1, columns), True, same)
    inc_other, around, line = lax.optimization_barrier((inc_other, around, line))

    whole = pl.BlockSpec(memory_space=pltpu.VMEM)
    diff, bases = pl.pallas_call(
        pack_kernel,
        out_shape=(
            jax.ShapeDtypeStruct((group - 1, rows, LANES), jnp.bfloat16),
            jax.ShapeDtypeStruct((4, rows, LANES), jnp.float32),
        ),
        in_specs=[whole] * (group + 3),
        out_specs=(whole,) * 2,
        compiler_params=pltpu.CompilerParams(vmem_limit_bytes=4 * 1024 * 1024),
        cost_estimate=pl.CostEstimate(
            flops=PACK_COST, bytes_accessed=8 * columns * 4, transcendentals=0
        ),
    )(base, *around, *line)
    diffs = [
        diff,
        move(diff, False, beside),
        move(diff, True, same),
        move(diff, True, beside),
    ]
    bases = [bases, move(bases, False, lambda m: m ^ 1)]
    diffs += [move(x, False, lambda m: m ^ 1) for x in diffs]

    vectors = mem_size * block_count
    return pl.pallas_call(
        functools.partial(product_kernel, group),
        out_shape=jax.ShapeDtypeStruct((1, columns), jnp.float32),
        in_specs=[pl.BlockSpec(memory_space=pltpu.SMEM)]
        + [whole] * 12
        + [pl.BlockSpec(memory_space=pltpu.HBM)],
        out_specs=whole,
        scratch_shapes=[
            pltpu.VMEM((slots, block_size, block_size), jnp.bfloat16),
            pltpu.VMEM((mem_size * (rows + 1), LANES), jnp.float32),
            pltpu.VMEM((2 * block_count, mem_size, block_size), jnp.bfloat16),
            pltpu.VMEM((slots - 1, vectors, block_size), jnp.bfloat16),
            pltpu.VMEM((vectors, block_size), jnp.float32),
            pltpu.SemaphoreType.DMA((slots,)),
        ],
        compiler_params=pltpu.CompilerParams(vmem_limit_bytes=VMEM_LIMIT),
    )(offsets.T, *bases, *diffs, increments, inc_other, taper)


def solution(mesh):
    return jax.shard_map(
        on_device,
        mesh=mesh,
        in_specs=(P("mem", "lon"), P("mem", "lon"), P("lon", None), P()),
        out_specs=P("mem", "lon"),
        check_vma=False,
    )
```

```python
import functools

import jax
import jax.numpy as jnp
from jax import lax
from jax.experimental import pallas as pl
from jax.experimental.pallas import tpu as pltpu
from jax.sharding import PartitionSpec as P

LANES = 128
SUB = 8
VMEM_LIMIT = 51 * 1024 * 1024
PACK_COST = 20_000_000_000


def split_kernel(base_ref, split_ref):
    base = base_ref[...]
    high = base.astype(jnp.bfloat16)
    rest = base - high.astype(jnp.float32)
    middle = rest.astype(jnp.bfloat16)
    split_ref[0] = high
    split_ref[1] = middle
    split_ref[2] = (rest - middle.astype(jnp.float32)).astype(jnp.bfloat16)


def joined(parts):
    high, middle, low = (part.astype(jnp.float32) for part in parts)
    return high + middle + low


def pack_kernel(split_ref, *refs):
    line, out_ref = refs[:-1], refs[-1]
    base = joined([split_ref[i] for i in range(3)])
    out_ref[0:3] = split_ref[...]
    for j, ref in enumerate(line):
        out_ref[3 + j] = (ref[...] - base).astype(jnp.bfloat16)


def product_kernel(group, off_ref, *refs):
    groups = refs[:8]
    inc_own, inc_other, taper_hbm, out_ref = refs[8:12]
    tiles, pert, picked_from, acc, sems = refs[12:]
    slots, block_size, _ = tiles.shape
    members = 4 * group
    rows = groups[0].shape[1]
    pitch = pert.shape[0] // members
    quarters = block_size // LANES
    block_count = rows // quarters
    copies = []
    for s in range(slots):
        copies.append(pltpu.make_async_copy(taper_hbm.at[s], tiles.at[s], sems.at[s]))
        copies[-1].start()

    def weigh(side, inc_ref):
        lines = [groups[4 * c + 2 * side + j] for c in range(2) for j in range(2)]

        def chunk(r, carry):
            at = pl.multiple_of(r * 2 * SUB, 2 * SUB)
            here = pl.ds(at, 2 * SUB)
            starts = [joined([ref[k, here, :] for k in range(3)]) for ref in lines]
            steps = [
                [ref[3 + k, here, :].astype(jnp.float32) for k in range(group - 1)]
                for ref in lines
            ]
            total = sum(step for line in steps for step in line) + group * sum(starts)
            mean = total * (1.0 / members)
            m = 0
            for start, line in zip(starts, steps):
                start = start - mean
                for value in [start] + [start + step for step in line]:
                    pert[pl.ds(m * pitch + at, 2 * SUB), :] = value
                    m += 1
            return carry

        lax.fori_loop(0, rows // (2 * SUB), chunk, 0, unroll=2)

        for i in range(block_count):
            for q in range(quarters):
                lanes = slice(q * LANES, (q + 1) * LANES)
                at = i * quarters + q
                inc = inc_ref[:, at * LANES : (at + 1) * LANES].astype(jnp.float32)
                part = pert[pl.ds(at, members, pitch), :] * inc
                picked_from[side * block_count + i, :, lanes] = part.astype(jnp.bfloat16)

    weigh(1, inc_other)
    weigh(0, inc_own)

    contract = (((1,), (1,)), ((), ()))
    vectors = block_count * members
    copies[0].wait()
    acc[...] = lax.dot_general(
        picked_from[0:block_count].reshape(vectors, block_size),
        tiles[0],
        contract,
        preferred_element_type=jnp.float32,
    )
    for s in range(1, slots):
        chosen = []
        for i in range(block_count):
            place = i + off_ref[s - 1, i]
            place = jnp.where(place < 0, place + 2 * block_count, place)
            chosen.append(picked_from[place])
        copies[s].wait()
        acc[...] += lax.dot_general(
            jnp.concatenate(chosen, axis=0),
            tiles[s],
            contract,
            preferred_element_type=jnp.float32,
        )

    scale = 1.0 / (members - 1)
    for i in range(block_count):
        for q in range(quarters):
            lanes = slice(q * LANES, (q + 1) * LANES)
            term = (
                pert[pl.ds(i * quarters + q, members, pitch), :]
                * acc[i * members : (i + 1) * members, lanes]
            )
            row = jnp.sum(term, axis=0, keepdims=True) * scale
            out_ref[:, i * block_size + q * LANES : i * block_size + (q + 1) * LANES] = row


def mover(lon_size, mem_size):
    def one(x, step, mem_of):
        perm = []
        for l in range(lon_size):
            for m in range(mem_size):
                source = ((l + step) % lon_size) * mem_size + mem_of(m)
                perm.append((source, l * mem_size + m))
        return lax.ppermute(x, ("lon", "mem"), perm)

    def move(x, across, mem_of):
        if not across:
            return one(x, 0, mem_of)
        if lon_size == 2:
            return one(x, 1, mem_of)
        axis = x.ndim - 2 if x.shape[-2] > 1 else x.ndim - 1
        right, left = jnp.split(x, 2, axis=axis)
        return jnp.concatenate([one(right, 1, mem_of), one(left, -1, mem_of)], axis=axis)

    return move


def on_device(ensemble, increments, offsets, taper):
    lon_size, mem_size = lax.axis_size("lon"), lax.axis_size("mem")
    group = mem_size // 4
    slots, block_size, _ = taper.shape
    block_count = offsets.shape[0]
    columns = ensemble.shape[1]
    rows = columns // LANES
    move = mover(lon_size, mem_size)
    same, beside = (lambda m: m), (lambda m: m ^ 2)

    base = ensemble.reshape(rows, LANES)
    line = [
        move(base, False, lambda m: (m + 4 * d) % mem_size) for d in reversed(range(1, group))
    ]
    inc_other = move(increments.reshape(1, columns), True, same)
    whole = pl.BlockSpec(memory_space=pltpu.VMEM)
    small = pltpu.CompilerParams(vmem_limit_bytes=4 * 1024 * 1024)
    split = pl.pallas_call(
        split_kernel,
        out_shape=jax.ShapeDtypeStruct((3, rows, LANES), jnp.bfloat16),
        in_specs=[whole],
        out_specs=whole,
        compiler_params=small,
    )(base)
    split, inc_other, line = lax.optimization_barrier((split, inc_other, line))

    mine = pl.pallas_call(
        pack_kernel,
        out_shape=jax.ShapeDtypeStruct((group + 2, rows, LANES), jnp.bfloat16),
        in_specs=[whole] * group,
        out_specs=whole,
        compiler_params=small,
        cost_estimate=pl.CostEstimate(
            flops=PACK_COST, bytes_accessed=8 * columns * 4, transcendentals=0
        ),
    )(split, *line)
    groups = [
        mine,
        move(mine, False, beside),
        move(mine, True, same),
        move(mine, True, beside),
    ]
    groups += [move(x, False, lambda m: m ^ 1) for x in groups]

    vectors = mem_size * block_count
    return pl.pallas_call(
        functools.partial(product_kernel, group),
        out_shape=jax.ShapeDtypeStruct((1, columns), jnp.float32),
        in_specs=[pl.BlockSpec(memory_space=pltpu.SMEM)]
        + [whole] * 10
        + [pl.BlockSpec(memory_space=pltpu.HBM)],
        out_specs=whole,
        scratch_shapes=[
            pltpu.VMEM((slots, block_size, block_size), jnp.bfloat16),
            pltpu.VMEM((mem_size * (rows + 1), LANES), jnp.float32),
            pltpu.VMEM((2 * block_count, mem_size, block_size), jnp.bfloat16),
            pltpu.VMEM((vectors, block_size), jnp.float32),
            pltpu.SemaphoreType.DMA((slots,)),
        ],
        compiler_params=pltpu.CompilerParams(vmem_limit_bytes=VMEM_LIMIT),
    )(offsets.T, *groups, increments, inc_other, taper)


def solution(mesh):
    return jax.shard_map(
        on_device,
        mesh=mesh,
        in_specs=(P("mem", "lon"), P("mem", "lon"), P("lon", None), P()),
        out_specs=P("mem", "lon"),
        check_vma=False,
    )
```

```python
import functools

import jax
import jax.numpy as jnp
from jax import lax
from jax.experimental import pallas as pl
from jax.experimental.pallas import tpu as pltpu
from jax.sharding import PartitionSpec as P

LANES = 128
SUB = 8
VMEM_LIMIT = 49 * 1024 * 1024
PACK_COST = 20_000_000_000
OWN_COST = 1_500_000_000


def split_kernel(base_ref, split_ref):
    base = base_ref[...]
    high = base.astype(jnp.bfloat16)
    rest = base - high.astype(jnp.float32)
    middle = rest.astype(jnp.bfloat16)
    split_ref[0] = high
    split_ref[1] = middle
    split_ref[2] = (rest - middle.astype(jnp.float32)).astype(jnp.bfloat16)


def joined(parts):
    high, middle, low = (part.astype(jnp.float32) for part in parts)
    return high + middle + low


def pack_kernel(split_ref, *refs):
    line, out_ref = refs[:-1], refs[-1]
    base = joined([split_ref[i] for i in range(3)])
    out_ref[0:3] = split_ref[...]
    for j, ref in enumerate(line):
        out_ref[3 + j] = (ref[...] - base).astype(jnp.bfloat16)


def state_rows(lines, here, group):
    starts = [joined([ref[k, here, :] for k in range(3)]) for ref in lines]
    steps = [[ref[3 + k, here, :].astype(jnp.float32) for k in range(group - 1)] for ref in lines]
    return starts, steps


def perturb_rows(lines, pert, group):
    members = 4 * group
    rows = lines[0].shape[1]
    pitch = pert.shape[0] // members

    def chunk(r, carry):
        at = pl.multiple_of(r * 2 * SUB, 2 * SUB)
        starts, steps = state_rows(lines, pl.ds(at, 2 * SUB), group)
        total = sum(step for line in steps for step in line) + group * sum(starts)
        mean = total * (1.0 / members)
        m = 0
        for start, line in zip(starts, steps):
            start = start - mean
            for value in [start] + [start + step for step in line]:
                pert[pl.ds(m * pitch + at, 2 * SUB), :] = value
                m += 1
        return carry

    lax.fori_loop(0, rows // (2 * SUB), chunk, 0, unroll=2)


def spread_rows(pert, members, inc_ref, weighted_ref, wide_ref=None):
    block_count, _, block_size = weighted_ref.shape
    pitch = pert.shape[0] // members
    for i in range(block_count):
        for q in range(block_size // LANES):
            lanes = slice(q * LANES, (q + 1) * LANES)
            at = i * (block_size // LANES) + q
            inc = inc_ref[:, at * LANES : (at + 1) * LANES].astype(jnp.float32)
            part = pert[pl.ds(at, members, pitch), :]
            if wide_ref is not None:
                wide_ref[i, :, lanes] = part
            weighted_ref[i, :, lanes] = (part * inc).astype(jnp.bfloat16)


CONTRACT = (((1,), (1,)), ((), ()))


def own_kernel(group, *refs):
    lines, (inc_ref, taper_hbm) = refs[:4], refs[4:6]
    weighted_ref, wide_ref, acc_ref, tile, pert, sem = refs[6:]
    block_count, members, block_size = weighted_ref.shape
    copy = pltpu.make_async_copy(taper_hbm.at[0], tile, sem)
    copy.start()
    perturb_rows(lines, pert, group)
    spread_rows(pert, members, inc_ref, weighted_ref, wide_ref)
    copy.wait()
    acc_ref[...] = lax.dot_general(
        weighted_ref[...].reshape(block_count * members, block_size),
        tile[...],
        CONTRACT,
        preferred_element_type=jnp.float32,
    )


def product_kernel(group, off_ref, *refs):
    own_ref, wide_ref, first_ref = refs[:3]
    lines, (inc_ref, taper_hbm, out_ref) = refs[3:7], refs[7:10]
    tiles, pert, picked_from, acc, sems = refs[10:]
    slots, block_size, _ = taper_hbm.shape
    block_count, members, _ = own_ref.shape
    copies = []
    for s in range(1, slots):
        copies.append(pltpu.make_async_copy(taper_hbm.at[s], tiles.at[s - 1], sems.at[s - 1]))
        copies[-1].start()

    picked_from[0:block_count] = own_ref[...]
    perturb_rows(lines, pert, group)
    spread_rows(pert, members, inc_ref, picked_from.at[pl.ds(block_count, block_count)])

    for s in range(1, slots):
        chosen = []
        for i in range(block_count):
            place = i + off_ref[s - 1, i]
            place = jnp.where(place < 0, place + 2 * block_count, place)
            chosen.append(picked_from[place])
        copies[s - 1].wait()
        so_far = first_ref[...] if s == 1 else acc[...]
        acc[...] = so_far + lax.dot_general(
            jnp.concatenate(chosen, axis=0),
            tiles[s - 1],
            CONTRACT,
            preferred_element_type=jnp.float32,
        )

    scale = 1.0 / (members - 1)
    for i in range(block_count):
        for q in range(block_size // LANES):
            lanes = slice(q * LANES, (q + 1) * LANES)
            term = wide_ref[i, :, lanes] * acc[i * members : (i + 1) * members, lanes]
            row = jnp.sum(term, axis=0, keepdims=True) * scale
            out_ref[:, i * block_size + q * LANES : i * block_size + (q + 1) * LANES] = row


def mover(lon_size, mem_size):
    def one(x, step, mem_of):
        perm = []
        for l in range(lon_size):
            for m in range(mem_size):
                source = ((l + step) % lon_size) * mem_size + mem_of(m)
                perm.append((source, l * mem_size + m))
        return lax.ppermute(x, ("lon", "mem"), perm)

    def move(x, across, mem_of):
        if not across:
            return one(x, 0, mem_of)
        if lon_size == 2:
            return one(x, 1, mem_of)
        axis = x.ndim - 2 if x.shape[-2] > 1 else x.ndim - 1
        right, left = jnp.split(x, 2, axis=axis)
        return jnp.concatenate([one(right, 1, mem_of), one(left, -1, mem_of)], axis=axis)

    return move


def on_device(ensemble, increments, offsets, taper):
    lon_size, mem_size = lax.axis_size("lon"), lax.axis_size("mem")
    group = mem_size // 4
    slots, block_size, _ = taper.shape
    block_count = offsets.shape[0]
    columns = ensemble.shape[1]
    rows = columns // LANES
    move = mover(lon_size, mem_size)
    same, beside = (lambda m: m), (lambda m: m ^ 2)

    base = ensemble.reshape(rows, LANES)
    if group & (group - 1):
        turn = lambda d: lambda m: (m + 4 * d) % mem_size
    else:
        turn = lambda d: lambda m: m ^ (4 * d)
    line = [move(base, False, turn(d)) for d in range(1, group)]
    inc_other = move(increments.reshape(1, columns), True, same)
    whole = pl.BlockSpec(memory_space=pltpu.VMEM)
    small = pltpu.CompilerParams(vmem_limit_bytes=4 * 1024 * 1024)
    split = pl.pallas_call(
        split_kernel,
        out_shape=jax.ShapeDtypeStruct((3, rows, LANES), jnp.bfloat16),
        in_specs=[whole],
        out_specs=whole,
        compiler_params=small,
    )(base)
    split, inc_other, line = lax.optimization_barrier((split, inc_other, line))

    mine = pl.pallas_call(
        pack_kernel,
        out_shape=jax.ShapeDtypeStruct((group + 2, rows, LANES), jnp.bfloat16),
        in_specs=[whole] * group,
        out_specs=whole,
        compiler_params=small,
        cost_estimate=pl.CostEstimate(
            flops=PACK_COST, bytes_accessed=8 * columns * 4, transcendentals=0
        ),
    )(split, *line)
    y = move(mine, True, same)
    diag = move(mine, True, beside)
    x = move(mine, False, beside)
    own = [mine, x] + [move(v, False, lambda m: m ^ 1) for v in (mine, x)]
    other = [y, diag] + [move(v, False, lambda m: m ^ 1) for v in (y, diag)]

    vectors = mem_size * block_count
    hbm = pl.BlockSpec(memory_space=pltpu.HBM)
    weighted, wide, first = pl.pallas_call(
        functools.partial(own_kernel, group),
        out_shape=(
            jax.ShapeDtypeStruct((block_count, mem_size, block_size), jnp.bfloat16),
            jax.ShapeDtypeStruct((block_count, mem_size, block_size), jnp.float32),
            jax.ShapeDtypeStruct((vectors, block_size), jnp.float32),
        ),
        in_specs=[whole] * 5 + [hbm],
        out_specs=(whole,) * 3,
        scratch_shapes=[
            pltpu.VMEM((block_size, block_size), jnp.bfloat16),
            pltpu.VMEM((mem_size * (rows + 1), LANES), jnp.float32),
            pltpu.SemaphoreType.DMA,
        ],
        compiler_params=pltpu.CompilerParams(vmem_limit_bytes=VMEM_LIMIT),
        cost_estimate=pl.CostEstimate(
            flops=OWN_COST, bytes_accessed=block_size * block_size * 2, transcendentals=0
        ),
    )(*own, increments, taper)
    return pl.pallas_call(
        functools.partial(product_kernel, group),
        out_shape=jax.ShapeDtypeStruct((1, columns), jnp.float32),
        in_specs=[pl.BlockSpec(memory_space=pltpu.SMEM)] + [whole] * 8 + [hbm],
        out_specs=whole,
        scratch_shapes=[
            pltpu.VMEM((slots - 1, block_size, block_size), jnp.bfloat16),
            pltpu.VMEM((mem_size * (rows + 1), LANES), jnp.float32),
            pltpu.VMEM((2 * block_count, mem_size, block_size), jnp.bfloat16),
            pltpu.VMEM((vectors, block_size), jnp.float32),
            pltpu.SemaphoreType.DMA((slots - 1,)),
        ],
        compiler_params=pltpu.CompilerParams(vmem_limit_bytes=VMEM_LIMIT),
    )(offsets.T, weighted, wide, first, *other, inc_other, taper)


def solution(mesh):
    return jax.shard_map(
        on_device,
        mesh=mesh,
        in_specs=(P("mem", "lon"), P("mem", "lon"), P("lon", None), P()),
        out_specs=P("mem", "lon"),
        check_vma=False,
    )
```

```python
import functools

import jax
import jax.numpy as jnp
from jax import lax
from jax.experimental import pallas as pl
from jax.experimental.pallas import tpu as pltpu
from jax.sharding import PartitionSpec as P

LANES = 128
SUB = 8
VMEM_LIMIT = 16 * 1024 * 1024
PACK_COST = 20_000_000_000


def split_kernel(base_ref, split_ref):
    base = base_ref[...]
    high = base.astype(jnp.bfloat16)
    rest = base - high.astype(jnp.float32)
    middle = rest.astype(jnp.bfloat16)
    split_ref[0] = high
    split_ref[1] = middle
    split_ref[2] = (rest - middle.astype(jnp.float32)).astype(jnp.bfloat16)


def joined(parts):
    high, middle, low = (part.astype(jnp.float32) for part in parts)
    return high + middle + low


def pack_kernel(split_ref, *refs):
    line, out_ref = refs[:-1], refs[-1]
    base = joined([split_ref[i] for i in range(3)])
    out_ref[0:3] = split_ref[...]
    for j, ref in enumerate(line):
        out_ref[3 + j] = (ref[...] - base).astype(jnp.bfloat16)


def product_kernel(group, off_ref, *refs):
    groups = refs[:8]
    inc_own, inc_other, tiles, out_ref = refs[8:12]
    pert, picked_from, acc = refs[12:]
    slots, block_size, _ = tiles.shape
    members = 4 * group
    rows = groups[0].shape[1]
    pitch = pert.shape[0] // members
    quarters = block_size // LANES
    block_count = rows // quarters

    def weigh(side, inc_ref):
        lines = [groups[4 * c + 2 * side + j] for c in range(2) for j in range(2)]

        def chunk(r, carry):
            at = pl.multiple_of(r * 2 * SUB, 2 * SUB)
            here = pl.ds(at, 2 * SUB)
            starts = [joined([ref[k, here, :] for k in range(3)]) for ref in lines]
            steps = [
                [ref[3 + k, here, :].astype(jnp.float32) for k in range(group - 1)]
                for ref in lines
            ]
            total = sum(step for line in steps for step in line) + group * sum(starts)
            mean = total * (1.0 / members)
            m = 0
            for start, line in zip(starts, steps):
                start = start - mean
                for value in [start] + [start + step for step in line]:
                    pert[pl.ds(m * pitch + at, 2 * SUB), :] = value
                    m += 1
            return carry

        lax.fori_loop(0, rows // (2 * SUB), chunk, 0, unroll=2)

        for i in range(block_count):
            for q in range(quarters):
                lanes = slice(q * LANES, (q + 1) * LANES)
                at = i * quarters + q
                inc = inc_ref[:, at * LANES : (at + 1) * LANES].astype(jnp.float32)
                part = pert[pl.ds(at, members, pitch), :] * inc
                picked_from[side * block_count + i, :, lanes] = part.astype(jnp.bfloat16)

    weigh(1, inc_other)
    weigh(0, inc_own)

    contract = (((1,), (1,)), ((), ()))
    vectors = block_count * members
    acc[...] = lax.dot_general(
        picked_from[0:block_count].reshape(vectors, block_size),
        tiles[0],
        contract,
        preferred_element_type=jnp.float32,
    )
    for s in range(1, slots):
        chosen = []
        for i in range(block_count):
            place = i + off_ref[s - 1, i]
            place = jnp.where(place < 0, place + 2 * block_count, place)
            chosen.append(picked_from[place])
        acc[...] += lax.dot_general(
            jnp.concatenate(chosen, axis=0),
            tiles[s],
            contract,
            preferred_element_type=jnp.float32,
        )

    scale = 1.0 / (members - 1)
    for i in range(block_count):
        for q in range(quarters):
            lanes = slice(q * LANES, (q + 1) * LANES)
            term = (
                pert[pl.ds(i * quarters + q, members, pitch), :]
                * acc[i * members : (i + 1) * members, lanes]
            )
            row = jnp.sum(term, axis=0, keepdims=True) * scale
            out_ref[:, i * block_size + q * LANES : i * block_size + (q + 1) * LANES] = row


def mover(lon_size, mem_size):
    def one(x, step, mem_of):
        perm = []
        for l in range(lon_size):
            for m in range(mem_size):
                source = ((l + step) % lon_size) * mem_size + mem_of(m)
                perm.append((source, l * mem_size + m))
        return lax.ppermute(x, ("lon", "mem"), perm)

    def move(x, across, mem_of):
        if not across:
            return one(x, 0, mem_of)
        if lon_size == 2:
            return one(x, 1, mem_of)
        axis = x.ndim - 2 if x.shape[-2] > 1 else x.ndim - 1
        right, left = jnp.split(x, 2, axis=axis)
        return jnp.concatenate([one(right, 1, mem_of), one(left, -1, mem_of)], axis=axis)

    return move


def on_device(ensemble, increments, offsets, taper):
    lon_size, mem_size = lax.axis_size("lon"), lax.axis_size("mem")
    group = mem_size // 4
    slots, block_size, _ = taper.shape
    block_count = offsets.shape[0]
    columns = ensemble.shape[1]
    rows = columns // LANES
    move = mover(lon_size, mem_size)
    same, beside = (lambda m: m), (lambda m: m ^ 2)

    base = ensemble.reshape(rows, LANES)
    if group & (group - 1):
        turn = lambda d: lambda m: (m + 4 * d) % mem_size
    else:
        turn = lambda d: lambda m: m ^ (4 * d)
    line = [move(base, False, turn(d)) for d in range(1, group)]
    inc_other = move(increments.reshape(1, columns), True, same)
    whole = pl.BlockSpec(memory_space=pltpu.VMEM)
    small = pltpu.CompilerParams(vmem_limit_bytes=4 * 1024 * 1024)
    split = pl.pallas_call(
        split_kernel,
        out_shape=jax.ShapeDtypeStruct((3, rows, LANES), jnp.bfloat16),
        in_specs=[whole],
        out_specs=whole,
        compiler_params=small,
    )(base)
    split, inc_other, line = lax.optimization_barrier((split, inc_other, line))

    mine = pl.pallas_call(
        pack_kernel,
        out_shape=jax.ShapeDtypeStruct((group + 2, rows, LANES), jnp.bfloat16),
        in_specs=[whole] * group,
        out_specs=whole,
        compiler_params=small,
        cost_estimate=pl.CostEstimate(
            flops=PACK_COST, bytes_accessed=8 * columns * 4, transcendentals=0
        ),
    )(split, *line)
    groups = [
        mine,
        move(mine, False, beside),
        move(mine, True, same),
        move(mine, True, beside),
    ]
    groups += [move(x, False, lambda m: m ^ 1) for x in groups]

    vectors = mem_size * block_count
    return pl.pallas_call(
        functools.partial(product_kernel, group),
        out_shape=jax.ShapeDtypeStruct((1, columns), jnp.float32),
        in_specs=[pl.BlockSpec(memory_space=pltpu.SMEM)] + [whole] * 11,
        out_specs=whole,
        scratch_shapes=[
            pltpu.VMEM((mem_size * (rows + 1), LANES), jnp.float32),
            pltpu.VMEM((2 * block_count, mem_size, block_size), jnp.bfloat16),
            pltpu.VMEM((vectors, block_size), jnp.float32),
        ],
        compiler_params=pltpu.CompilerParams(vmem_limit_bytes=VMEM_LIMIT),
    )(offsets.T, *groups, increments, inc_other, taper)


def solution(mesh):
    return jax.shard_map(
        on_device,
        mesh=mesh,
        in_specs=(P("mem", "lon"), P("mem", "lon"), P("lon", None), P()),
        out_specs=P("mem", "lon"),
        check_vma=False,
    )
```

```python
import functools

import jax
import jax.numpy as jnp
from jax import lax
from jax.experimental import pallas as pl
from jax.experimental.pallas import tpu as pltpu
from jax.sharding import PartitionSpec as P

LANES = 128
SUB = 8
VMEM_LIMIT = 16 * 1024 * 1024
PACK_COST = 20_000_000_000


def pair_kernel(base_ref, inc_ref, pair_ref):
    pair_ref[0] = base_ref[...]
    for r in range(base_ref.shape[0]):
        part = inc_ref[:, r * LANES : (r + 1) * LANES]
        pair_ref[1, r : r + 1, :] = part.astype(jnp.float32)


def pack_kernel(pair_ref, *refs):
    line, (diff_ref, mine_ref) = refs[:-2], refs[-2:]
    base = pair_ref[0]
    high = base.astype(jnp.bfloat16)
    rest = base - high.astype(jnp.float32)
    middle = rest.astype(jnp.bfloat16)
    mine_ref[0] = high
    mine_ref[1] = middle
    mine_ref[2] = (rest - middle.astype(jnp.float32)).astype(jnp.bfloat16)
    for j, ref in enumerate(line):
        step = (ref[...] - base).astype(jnp.bfloat16)
        diff_ref[j] = step
        mine_ref[3 + j] = step


def product_kernel(group, off_ref, *refs):
    half = len(refs[:14]) // 2
    cores = refs[:half], refs[half : 2 * half]
    inc_own, inc_other = refs[14], refs[3]
    tiles, out_ref = refs[15:17]
    pert, picked_from, acc = refs[17:]
    slots, block_size, _ = tiles.shape
    members = 4 * group
    rows = inc_other.shape[1]
    pitch = pert.shape[0] // members
    quarters = block_size // LANES
    block_count = rows // quarters

    def weigh(side, increment):
        if side == 0:
            lines = [pair for core in cores for pair in ((None, core[0]), core[1:3])]
        else:
            lines = [pair for core in cores for pair in (core[3:5], core[5:7])]

        def chunk(r, carry):
            at = pl.multiple_of(r * 2 * SUB, 2 * SUB)
            here = pl.ds(at, 2 * SUB)
            starts, steps = [], []
            for base, ref in lines:
                if base is None:
                    high, middle, low = (ref[k, here, :].astype(jnp.float32) for k in range(3))
                    starts.append(high + middle + low)
                else:
                    starts.append(base[0, here, :])
                first = ref.shape[0] - (group - 1)
                steps.append(
                    [ref[first + k, here, :].astype(jnp.float32) for k in range(group - 1)]
                )
            total = sum(step for line in steps for step in line) + group * sum(starts)
            mean = total * (1.0 / members)
            m = 0
            for start, line in zip(starts, steps):
                start = start - mean
                for value in [start] + [start + step for step in line]:
                    pert[pl.ds(m * pitch + at, 2 * SUB), :] = value
                    m += 1
            return carry

        lax.fori_loop(0, rows // (2 * SUB), chunk, 0, unroll=2)

        for i in range(block_count):
            for q in range(quarters):
                lanes = slice(q * LANES, (q + 1) * LANES)
                at = i * quarters + q
                part = pert[pl.ds(at, members, pitch), :] * increment(at)
                picked_from[side * block_count + i, :, lanes] = part.astype(jnp.bfloat16)

    weigh(1, lambda at: inc_other[1, at : at + 1, :])
    weigh(0, lambda at: inc_own[1, at : at + 1, :])

    contract = (((1,), (1,)), ((), ()))
    vectors = block_count * members
    acc[...] = lax.dot_general(
        picked_from[0:block_count].reshape(vectors, block_size),
        tiles[0],
        contract,
        preferred_element_type=jnp.float32,
    )
    for s in range(1, slots):
        chosen = []
        for i in range(block_count):
            place = i + off_ref[s - 1, i]
            place = jnp.where(place < 0, place + 2 * block_count, place)
            chosen.append(picked_from[place])
        acc[...] += lax.dot_general(
            jnp.concatenate(chosen, axis=0),
            tiles[s],
            contract,
            preferred_element_type=jnp.float32,
        )

    scale = 1.0 / (members - 1)
    for i in range(block_count):
        for q in range(quarters):
            lanes = slice(q * LANES, (q + 1) * LANES)
            term = (
                pert[pl.ds(i * quarters + q, members, pitch), :]
                * acc[i * members : (i + 1) * members, lanes]
            )
            row = jnp.sum(term, axis=0, keepdims=True) * scale
            out_ref[:, i * block_size + q * LANES : i * block_size + (q + 1) * LANES] = row


def mover(lon_size, mem_size):
    def one(x, step, mem_of):
        perm = []
        for l in range(lon_size):
            for m in range(mem_size):
                source = ((l + step) % lon_size) * mem_size + mem_of(m)
                perm.append((source, l * mem_size + m))
        return lax.ppermute(x, ("lon", "mem"), perm)

    def move(x, across, mem_of):
        if not across:
            return one(x, 0, mem_of)
        if lon_size == 2:
            return one(x, 1, mem_of)
        axis = x.ndim - 2 if x.shape[-2] > 1 else x.ndim - 1
        right, left = jnp.split(x, 2, axis=axis)
        return jnp.concatenate([one(right, 1, mem_of), one(left, -1, mem_of)], axis=axis)

    return move


def on_device(ensemble, increments, offsets, taper):
    lon_size, mem_size = lax.axis_size("lon"), lax.axis_size("mem")
    group = mem_size // 4
    slots, block_size, _ = taper.shape
    block_count = offsets.shape[0]
    columns = ensemble.shape[1]
    rows = columns // LANES
    move = mover(lon_size, mem_size)
    same, beside = (lambda m: m), (lambda m: m ^ 2)

    base = ensemble.reshape(rows, LANES)
    if group & (group - 1):
        turn = lambda d: lambda m: (m + 4 * d) % mem_size
    else:
        turn = lambda d: lambda m: m ^ (4 * d)
    line = [move(base, False, turn(d)) for d in range(1, group)]
    whole = pl.BlockSpec(memory_space=pltpu.VMEM)
    small = pltpu.CompilerParams(vmem_limit_bytes=4 * 1024 * 1024)
    pair = pl.pallas_call(
        pair_kernel,
        out_shape=jax.ShapeDtypeStruct((2, rows, LANES), jnp.float32),
        in_specs=[whole] * 2,
        out_specs=whole,
        compiler_params=small,
    )(base, increments)
    base_x = move(base[None], False, beside)
    base_diag = move(base[None], True, beside)
    base_y = move(pair, True, same)
    pair, line = lax.optimization_barrier((pair, line))

    diff, mine = pl.pallas_call(
        pack_kernel,
        out_shape=(
            jax.ShapeDtypeStruct((group - 1, rows, LANES), jnp.bfloat16),
            jax.ShapeDtypeStruct((group + 2, rows, LANES), jnp.bfloat16),
        ),
        in_specs=[whole] * group,
        out_specs=(whole, whole),
        compiler_params=small,
        cost_estimate=pl.CostEstimate(
            flops=PACK_COST, bytes_accessed=8 * columns * 4, transcendentals=0
        ),
    )(pair, *line)
    x, y = move(diff, False, beside), move(diff, True, same)
    diag = move(diff, True, beside)
    mine, base_x, base_y, base_diag = lax.optimization_barrier((mine, base_x, base_y, base_diag))
    lines = [mine, base_x, x, base_y, y, base_diag, diag]
    lines += [move(v, False, lambda m: m ^ 1) for v in lines]

    vectors = mem_size * block_count
    return pl.pallas_call(
        functools.partial(product_kernel, group),
        out_shape=jax.ShapeDtypeStruct((1, columns), jnp.float32),
        in_specs=[pl.BlockSpec(memory_space=pltpu.SMEM)] + [whole] * 16,
        out_specs=whole,
        scratch_shapes=[
            pltpu.VMEM((mem_size * (rows + 1), LANES), jnp.float32),
            pltpu.VMEM((2 * block_count, mem_size, block_size), jnp.bfloat16),
            pltpu.VMEM((vectors, block_size), jnp.float32),
        ],
        compiler_params=pltpu.CompilerParams(vmem_limit_bytes=VMEM_LIMIT),
    )(offsets.T, *lines, pair, taper)


def solution(mesh):
    return jax.shard_map(
        on_device,
        mesh=mesh,
        in_specs=(P("mem", "lon"), P("mem", "lon"), P("lon", None), P()),
        out_specs=P("mem", "lon"),
        check_vma=False,
    )
```

```python
import functools

import jax
import jax.numpy as jnp
from jax import lax
from jax.experimental import pallas as pl
from jax.experimental.pallas import tpu as pltpu
from jax.sharding import PartitionSpec as P

LANES = 128
SUB = 8
VMEM_LIMIT = 16 * 1024 * 1024
PACK_COST = 20_000_000_000
FIRST_COST = 2_000_000_000


def first_kernel(out_ref):
    out_ref[...] = jnp.zeros_like(out_ref)


def bases_kernel(x_ref, y_ref, diag_ref, out_ref):
    for j, ref in enumerate((x_ref, y_ref, diag_ref)):
        out_ref[j] = ref[0]


def pair_kernel(first_ref, base_ref, inc_ref, pair_ref):
    pair_ref[0] = base_ref[...]
    for r in range(base_ref.shape[0]):
        part = inc_ref[:, r * LANES : (r + 1) * LANES]
        pair_ref[1, r : r + 1, :] = part.astype(jnp.float32)


def pack_kernel(pair_ref, *refs):
    line, (diff_ref, mine_ref) = refs[:-2], refs[-2:]
    base = pair_ref[0]
    high = base.astype(jnp.bfloat16)
    rest = base - high.astype(jnp.float32)
    middle = rest.astype(jnp.bfloat16)
    mine_ref[0] = high
    mine_ref[1] = middle
    mine_ref[2] = (rest - middle.astype(jnp.float32)).astype(jnp.bfloat16)
    for j, ref in enumerate(line):
        step = (ref[...] - base).astype(jnp.bfloat16)
        diff_ref[j] = step
        mine_ref[3 + j] = step


def product_kernel(group, off_ref, *refs):
    cores = refs[:5], refs[5:10]
    inc_other, inc_own, tiles, out_ref = refs[10:14]
    pert, picked_from, acc = refs[14:]
    slots, block_size, _ = tiles.shape
    members = 4 * group
    rows = inc_other.shape[1]
    pitch = pert.shape[0] // members
    quarters = block_size // LANES
    block_count = rows // quarters

    def weigh(side, increment):
        if side == 0:
            lines = [pair for core in cores for pair in ((None, core[0]), (core[1].at[0], core[2]))]
        else:
            lines = [
                (core[1].at[j], core[2 + j]) for core in cores for j in (1, 2)
            ]

        def chunk(r, carry):
            at = pl.multiple_of(r * 2 * SUB, 2 * SUB)
            here = pl.ds(at, 2 * SUB)
            starts, steps = [], []
            for base, ref in lines:
                if base is None:
                    high, middle, low = (ref[k, here, :].astype(jnp.float32) for k in range(3))
                    starts.append(high + middle + low)
                else:
                    starts.append(base[here, :])
                first = ref.shape[0] - (group - 1)
                steps.append(
                    [ref[first + k, here, :].astype(jnp.float32) for k in range(group - 1)]
                )
            total = sum(step for line in steps for step in line) + group * sum(starts)
            mean = total * (1.0 / members)
            m = 0
            for start, line in zip(starts, steps):
                start = start - mean
                for value in [start] + [start + step for step in line]:
                    pert[pl.ds(m * pitch + at, 2 * SUB), :] = value
                    m += 1
            return carry

        lax.fori_loop(0, rows // (2 * SUB), chunk, 0, unroll=2)

        for i in range(block_count):
            for q in range(quarters):
                lanes = slice(q * LANES, (q + 1) * LANES)
                at = i * quarters + q
                part = pert[pl.ds(at, members, pitch), :] * increment(at)
                picked_from[side * block_count + i, :, lanes] = part.astype(jnp.bfloat16)

    weigh(1, lambda at: inc_other[1, at : at + 1, :])
    weigh(0, lambda at: inc_own[1, at : at + 1, :])

    contract = (((1,), (1,)), ((), ()))
    vectors = block_count * members
    acc[...] = lax.dot_general(
        picked_from[0:block_count].reshape(vectors, block_size),
        tiles[0],
        contract,
        preferred_element_type=jnp.float32,
    )
    for s in range(1, slots):
        chosen = []
        for i in range(block_count):
            place = i + off_ref[s - 1, i]
            place = jnp.where(place < 0, place + 2 * block_count, place)
            chosen.append(picked_from[place])
        acc[...] += lax.dot_general(
            jnp.concatenate(chosen, axis=0),
            tiles[s],
            contract,
            preferred_element_type=jnp.float32,
        )

    scale = 1.0 / (members - 1)
    for i in range(block_count):
        for q in range(quarters):
            lanes = slice(q * LANES, (q + 1) * LANES)
            term = (
                pert[pl.ds(i * quarters + q, members, pitch), :]
                * acc[i * members : (i + 1) * members, lanes]
            )
            row = jnp.sum(term, axis=0, keepdims=True) * scale
            out_ref[:, i * block_size + q * LANES : i * block_size + (q + 1) * LANES] = row


def mover(lon_size, mem_size):
    def one(x, step, mem_of):
        perm = []
        for l in range(lon_size):
            for m in range(mem_size):
                source = ((l + step) % lon_size) * mem_size + mem_of(m)
                perm.append((source, l * mem_size + m))
        return lax.ppermute(x, ("lon", "mem"), perm)

    def move(x, across, mem_of):
        if not across:
            return one(x, 0, mem_of)
        if lon_size == 2:
            return one(x, 1, mem_of)
        axis = x.ndim - 2 if x.shape[-2] > 1 else x.ndim - 1
        right, left = jnp.split(x, 2, axis=axis)
        return jnp.concatenate([one(right, 1, mem_of), one(left, -1, mem_of)], axis=axis)

    return move


def on_device(ensemble, increments, offsets, taper):
    lon_size, mem_size = lax.axis_size("lon"), lax.axis_size("mem")
    group = mem_size // 4
    slots, block_size, _ = taper.shape
    block_count = offsets.shape[0]
    columns = ensemble.shape[1]
    rows = columns // LANES
    move = mover(lon_size, mem_size)
    same, beside = (lambda m: m), (lambda m: m ^ 2)

    base = ensemble.reshape(rows, LANES)
    if group & (group - 1):
        turn = lambda d: lambda m: (m + 4 * d) % mem_size
    else:
        turn = lambda d: lambda m: m ^ (4 * d)
    line = [move(base, False, turn(d)) for d in range(1, group)]
    whole = pl.BlockSpec(memory_space=pltpu.VMEM)
    small = pltpu.CompilerParams(vmem_limit_bytes=4 * 1024 * 1024)
    first = pl.pallas_call(
        first_kernel,
        out_shape=jax.ShapeDtypeStruct((SUB, LANES), jnp.float32),
        out_specs=whole,
        compiler_params=small,
        cost_estimate=pl.CostEstimate(flops=FIRST_COST, bytes_accessed=4096, transcendentals=0),
    )()
    pair = pl.pallas_call(
        pair_kernel,
        out_shape=jax.ShapeDtypeStruct((2, rows, LANES), jnp.float32),
        in_specs=[whole] * 3,
        out_specs=whole,
        compiler_params=small,
    )(first, base, increments)
    later, _ = lax.optimization_barrier((base, first))
    base_x = move(later[None], False, beside)
    base_diag = move(later[None], True, beside)
    base_y = move(pair, True, same)
    pair, line = lax.optimization_barrier((pair, line))

    diff, mine = pl.pallas_call(
        pack_kernel,
        out_shape=(
            jax.ShapeDtypeStruct((group - 1, rows, LANES), jnp.bfloat16),
            jax.ShapeDtypeStruct((group + 2, rows, LANES), jnp.bfloat16),
        ),
        in_specs=[whole] * group,
        out_specs=(whole, whole),
        compiler_params=small,
        cost_estimate=pl.CostEstimate(
            flops=PACK_COST, bytes_accessed=8 * columns * 4, transcendentals=0
        ),
    )(pair, *line)
    x, y = move(diff, False, beside), move(diff, True, same)
    diag = move(diff, True, beside)
    mine, base_x, base_y, base_diag = lax.optimization_barrier((mine, base_x, base_y, base_diag))
    bases = pl.pallas_call(
        bases_kernel,
        out_shape=jax.ShapeDtypeStruct((3, rows, LANES), jnp.float32),
        in_specs=[whole] * 3,
        out_specs=whole,
        compiler_params=small,
    )(base_x, base_y, base_diag)
    lines = [mine, bases, x, y, diag]
    lines += [move(v, False, lambda m: m ^ 1) for v in lines]

    vectors = mem_size * block_count
    return pl.pallas_call(
        functools.partial(product_kernel, group),
        out_shape=jax.ShapeDtypeStruct((1, columns), jnp.float32),
        in_specs=[pl.BlockSpec(memory_space=pltpu.SMEM)] + [whole] * 13,
        out_specs=whole,
        scratch_shapes=[
            pltpu.VMEM((mem_size * (rows + 1), LANES), jnp.float32),
            pltpu.VMEM((2 * block_count, mem_size, block_size), jnp.bfloat16),
            pltpu.VMEM((vectors, block_size), jnp.float32),
        ],
        compiler_params=pltpu.CompilerParams(vmem_limit_bytes=VMEM_LIMIT),
    )(offsets.T, *lines, base_y, pair, taper)


def solution(mesh):
    return jax.shard_map(
        on_device,
        mesh=mesh,
        in_specs=(P("mem", "lon"), P("mem", "lon"), P("lon", None), P()),
        out_specs=P("mem", "lon"),
        check_vma=False,
    )
```

```python
import functools

import jax
import jax.numpy as jnp
from jax import lax
from jax.experimental import pallas as pl
from jax.experimental.pallas import tpu as pltpu
from jax.sharding import PartitionSpec as P

LANES = 128
SUB = 8
VMEM_LIMIT = 16 * 1024 * 1024
PACK_COST = 20_000_000_000
FIRST_COST = 2_000_000_000


def first_kernel(out_ref):
    out_ref[...] = jnp.zeros_like(out_ref)


def bases_kernel(x_ref, y_ref, diag_ref, out_ref):
    for j, ref in enumerate((x_ref, y_ref, diag_ref)):
        out_ref[j] = ref[0]


def pair_kernel(first_ref, base_ref, inc_ref, pair_ref):
    pair_ref[0] = base_ref[...]
    for r in range(base_ref.shape[0]):
        part = inc_ref[:, r * LANES : (r + 1) * LANES]
        pair_ref[1, r : r + 1, :] = part.astype(jnp.float32)


def pack_kernel(pair_ref, *refs):
    line, (diff_ref, mine_ref) = refs[:-2], refs[-2:]
    base = pair_ref[0]
    high = base.astype(jnp.bfloat16)
    rest = base - high.astype(jnp.float32)
    middle = rest.astype(jnp.bfloat16)
    mine_ref[0] = high
    mine_ref[1] = middle
    mine_ref[2] = (rest - middle.astype(jnp.float32)).astype(jnp.bfloat16)
    for j, ref in enumerate(line):
        step = (ref[...] - base).astype(jnp.bfloat16)
        diff_ref[j] = step
        mine_ref[3 + j] = step


def product_kernel(group, off_ref, *refs):
    cores = refs[:5], refs[5:10]
    inc_other, inc_own, tiles, out_ref = refs[10:14]
    pert, pert_other, picked_from, acc = refs[14:]
    slots, block_size, _ = tiles.shape
    members = 4 * group
    rows = inc_other.shape[1]
    pitch = pert.shape[0] // members
    quarters = block_size // LANES
    block_count = rows // quarters

    def weigh(side, pert, increment):
        if side == 0:
            lines = [pair for core in cores for pair in ((None, core[0]), (core[1].at[0], core[2]))]
        else:
            lines = [
                (core[1].at[j], core[2 + j]) for core in cores for j in (1, 2)
            ]

        def chunk(r):
            at = r * 2 * SUB
            here = pl.ds(at, 2 * SUB)
            starts, steps = [], []
            for base, ref in lines:
                if base is None:
                    high, middle, low = (ref[k, here, :].astype(jnp.float32) for k in range(3))
                    starts.append(high + middle + low)
                else:
                    starts.append(base[here, :])
                first = ref.shape[0] - (group - 1)
                steps.append(
                    [ref[first + k, here, :].astype(jnp.float32) for k in range(group - 1)]
                )
            total = sum(step for line in steps for step in line) + group * sum(starts)
            mean = total * (1.0 / members)
            m = 0
            for start, line in zip(starts, steps):
                start = start - mean
                for value in [start] + [start + step for step in line]:
                    pert[pl.ds(m * pitch + at, 2 * SUB), :] = value
                    m += 1

        for r in range(rows // (2 * SUB)):
            chunk(r)

        for i in range(block_count):
            for q in range(quarters):
                lanes = slice(q * LANES, (q + 1) * LANES)
                at = i * quarters + q
                part = pert[pl.ds(at, members, pitch), :] * increment(at)
                picked_from[side * block_count + i, :, lanes] = part.astype(jnp.bfloat16)

    weigh(0, pert, lambda at: inc_own[1, at : at + 1, :])

    contract = (((1,), (1,)), ((), ()))
    vectors = block_count * members
    acc[...] = lax.dot_general(
        picked_from[0:block_count].reshape(vectors, block_size),
        tiles[0],
        contract,
        preferred_element_type=jnp.float32,
    )
    weigh(1, pert_other, lambda at: inc_other[1, at : at + 1, :])
    for s in range(1, slots):
        chosen = []
        for i in range(block_count):
            place = i + off_ref[s - 1, i]
            place = jnp.where(place < 0, place + 2 * block_count, place)
            chosen.append(picked_from[place])
        acc[...] += lax.dot_general(
            jnp.concatenate(chosen, axis=0),
            tiles[s],
            contract,
            preferred_element_type=jnp.float32,
        )

    scale = 1.0 / (members - 1)
    for i in range(block_count):
        for q in range(quarters):
            lanes = slice(q * LANES, (q + 1) * LANES)
            term = (
                pert[pl.ds(i * quarters + q, members, pitch), :]
                * acc[i * members : (i + 1) * members, lanes]
            )
            row = jnp.sum(term, axis=0, keepdims=True) * scale
            out_ref[:, i * block_size + q * LANES : i * block_size + (q + 1) * LANES] = row


def mover(lon_size, mem_size):
    def one(x, step, mem_of):
        perm = []
        for l in range(lon_size):
            for m in range(mem_size):
                source = ((l + step) % lon_size) * mem_size + mem_of(m)
                perm.append((source, l * mem_size + m))
        return lax.ppermute(x, ("lon", "mem"), perm)

    def move(x, across, mem_of):
        if not across:
            return one(x, 0, mem_of)
        if lon_size == 2:
            return one(x, 1, mem_of)
        axis = x.ndim - 2 if x.shape[-2] > 1 else x.ndim - 1
        right, left = jnp.split(x, 2, axis=axis)
        return jnp.concatenate([one(right, 1, mem_of), one(left, -1, mem_of)], axis=axis)

    return move


def on_device(ensemble, increments, offsets, taper):
    lon_size, mem_size = lax.axis_size("lon"), lax.axis_size("mem")
    group = mem_size // 4
    slots, block_size, _ = taper.shape
    block_count = offsets.shape[0]
    columns = ensemble.shape[1]
    rows = columns // LANES
    move = mover(lon_size, mem_size)
    same, beside = (lambda m: m), (lambda m: m ^ 2)

    base = ensemble.reshape(rows, LANES)
    if group & (group - 1):
        turn = lambda d: lambda m: (m + 4 * d) % mem_size
    else:
        turn = lambda d: lambda m: m ^ (4 * d)
    line = [move(base, False, turn(d)) for d in range(1, group)]
    whole = pl.BlockSpec(memory_space=pltpu.VMEM)
    small = pltpu.CompilerParams(vmem_limit_bytes=4 * 1024 * 1024)
    first = pl.pallas_call(
        first_kernel,
        out_shape=jax.ShapeDtypeStruct((SUB, LANES), jnp.float32),
        out_specs=whole,
        compiler_params=small,
        cost_estimate=pl.CostEstimate(flops=FIRST_COST, bytes_accessed=4096, transcendentals=0),
    )()
    pair = pl.pallas_call(
        pair_kernel,
        out_shape=jax.ShapeDtypeStruct((2, rows, LANES), jnp.float32),
        in_specs=[whole] * 3,
        out_specs=whole,
        compiler_params=small,
    )(first, base, increments)
    later, _ = lax.optimization_barrier((base, first))
    base_x = move(later[None], False, beside)
    base_diag = move(later[None], True, beside)
    base_y = move(pair, True, same)
    pair, line = lax.optimization_barrier((pair, line))

    diff, mine = pl.pallas_call(
        pack_kernel,
        out_shape=(
            jax.ShapeDtypeStruct((group - 1, rows, LANES), jnp.bfloat16),
            jax.ShapeDtypeStruct((group + 2, rows, LANES), jnp.bfloat16),
        ),
        in_specs=[whole] * group,
        out_specs=(whole, whole),
        compiler_params=small,
        cost_estimate=pl.CostEstimate(
            flops=PACK_COST, bytes_accessed=8 * columns * 4, transcendentals=0
        ),
    )(pair, *line)
    x, y = move(diff, False, beside), move(diff, True, same)
    diag = move(diff, True, beside)
    mine, base_x, base_y, base_diag = lax.optimization_barrier((mine, base_x, base_y, base_diag))
    bases = pl.pallas_call(
        bases_kernel,
        out_shape=jax.ShapeDtypeStruct((3, rows, LANES), jnp.float32),
        in_specs=[whole] * 3,
        out_specs=whole,
        compiler_params=small,
    )(base_x, base_y, base_diag)
    lines = [mine, bases, x, y, diag]
    lines += [move(v, False, lambda m: m ^ 1) for v in lines]

    vectors = mem_size * block_count
    return pl.pallas_call(
        functools.partial(product_kernel, group),
        out_shape=jax.ShapeDtypeStruct((1, columns), jnp.float32),
        in_specs=[pl.BlockSpec(memory_space=pltpu.SMEM)] + [whole] * 13,
        out_specs=whole,
        scratch_shapes=[
            pltpu.VMEM((mem_size * (rows + 1), LANES), jnp.float32),
            pltpu.VMEM((mem_size * (rows + 1), LANES), jnp.float32),
            pltpu.VMEM((2 * block_count, mem_size, block_size), jnp.bfloat16),
            pltpu.VMEM((vectors, block_size), jnp.float32),
        ],
        compiler_params=pltpu.CompilerParams(vmem_limit_bytes=VMEM_LIMIT),
    )(offsets.T, *lines, base_y, pair, taper)


def solution(mesh):
    return jax.shard_map(
        on_device,
        mesh=mesh,
        in_specs=(P("mem", "lon"), P("mem", "lon"), P("lon", None), P()),
        out_specs=P("mem", "lon"),
        check_vma=False,
    )
```

```python
import functools

import jax
import jax.numpy as jnp
from jax import lax
from jax.experimental import pallas as pl
from jax.experimental.pallas import tpu as pltpu
from jax.sharding import PartitionSpec as P

LANES = 128
SUB = 8
VMEM_LIMIT = 16 * 1024 * 1024
PACK_COST = 20_000_000_000
FIRST_COST = 2_000_000_000


def first_kernel(out_ref):
    out_ref[...] = jnp.zeros_like(out_ref)


def pair_kernel(first_ref, base_ref, inc_ref, pair_ref):
    pair_ref[0] = base_ref[...]
    for r in range(base_ref.shape[0]):
        part = inc_ref[:, r * LANES : (r + 1) * LANES]
        pair_ref[1, r : r + 1, :] = part.astype(jnp.float32)


def pack_kernel(pair_ref, *refs):
    line, diff_ref = refs[:-1], refs[-1]
    for j, ref in enumerate(line):
        diff_ref[j] = (ref[...] - pair_ref[0]).astype(jnp.bfloat16)


def bundle_kernel(base_ref, diff_ref, out_ref):
    base = base_ref[0]
    high = base.astype(jnp.bfloat16)
    rest = base - high.astype(jnp.float32)
    middle = rest.astype(jnp.bfloat16)
    out_ref[0] = high
    out_ref[1] = middle
    out_ref[2] = (rest - middle.astype(jnp.float32)).astype(jnp.bfloat16)
    for j in range(diff_ref.shape[0]):
        out_ref[3 + j] = diff_ref[j]


def weigh(lines, group, inc_ref, pert, products):
    members = 4 * group
    pitch = pert.shape[0] // members
    block_count, _, block_size = products.shape
    quarters = block_size // LANES
    for at in range(0, block_count * quarters, 2 * SUB):
        here = slice(at, at + 2 * SUB)
        starts, steps = [], []
        for ref in lines:
            parts = [ref[k, here, :].astype(jnp.float32) for k in range(group + 2)]
            starts.append(parts[0] + parts[1] + parts[2])
            steps.append(parts[3:])
        total = sum(step for line in steps for step in line) + group * sum(starts)
        mean = total * (1.0 / members)
        m = 0
        for start, line in zip(starts, steps):
            start = start - mean
            for value in [start] + [start + step for step in line]:
                pert[pl.ds(m * pitch + at, 2 * SUB), :] = value
                m += 1
    for i in range(block_count):
        for q in range(quarters):
            at = i * quarters + q
            part = pert[pl.ds(at, members, pitch), :] * inc_ref[1, at : at + 1, :]
            products[i, :, q * LANES : (q + 1) * LANES] = part.astype(jnp.bfloat16)


def product_kernel(group, off_ref, *refs):
    own, other, (inc_own, inc_other, tiles, out_ref) = refs[:4], refs[4:8], refs[8:12]
    pert, pert_other, picked_from, acc = refs[12:]
    slots, block_size, _ = tiles.shape
    block_count, members = picked_from.shape[0] // 2, picked_from.shape[1]
    pitch = pert.shape[0] // members
    quarters = block_size // LANES
    weigh(own, group, inc_own, pert, picked_from.at[pl.ds(0, block_count)])

    contract = (((1,), (1,)), ((), ()))
    vectors = block_count * members
    acc[...] = lax.dot_general(
        picked_from[0:block_count].reshape(vectors, block_size),
        tiles[0],
        contract,
        preferred_element_type=jnp.float32,
    )
    weigh(other, group, inc_other, pert_other, picked_from.at[pl.ds(block_count, block_count)])
    for s in range(1, slots):
        chosen = []
        for i in range(block_count):
            place = i + off_ref[s - 1, i]
            place = jnp.where(place < 0, place + 2 * block_count, place)
            chosen.append(picked_from[place])
        acc[...] += lax.dot_general(
            jnp.concatenate(chosen, axis=0),
            tiles[s],
            contract,
            preferred_element_type=jnp.float32,
        )

    scale = 1.0 / (members - 1)
    for i in range(block_count):
        for q in range(quarters):
            lanes = slice(q * LANES, (q + 1) * LANES)
            term = (
                pert[pl.ds(i * quarters + q, members, pitch), :]
                * acc[i * members : (i + 1) * members, lanes]
            )
            row = jnp.sum(term, axis=0, keepdims=True) * scale
            out_ref[:, i * block_size + q * LANES : i * block_size + (q + 1) * LANES] = row


def mover(lon_size, mem_size):
    def one(x, step, mem_of):
        perm = []
        for l in range(lon_size):
            for m in range(mem_size):
                source = ((l + step) % lon_size) * mem_size + mem_of(m)
                perm.append((source, l * mem_size + m))
        return lax.ppermute(x, ("lon", "mem"), perm)

    def move(x, across, mem_of):
        if not across:
            return one(x, 0, mem_of)
        if lon_size == 2:
            return one(x, 1, mem_of)
        axis = x.ndim - 2 if x.shape[-2] > 1 else x.ndim - 1
        right, left = jnp.split(x, 2, axis=axis)
        return jnp.concatenate([one(right, 1, mem_of), one(left, -1, mem_of)], axis=axis)

    return move


def on_device(ensemble, increments, offsets, taper):
    lon_size, mem_size = lax.axis_size("lon"), lax.axis_size("mem")
    group = mem_size // 4
    slots, block_size, _ = taper.shape
    block_count = offsets.shape[0]
    columns = ensemble.shape[1]
    rows = columns // LANES
    move = mover(lon_size, mem_size)
    same, beside = (lambda m: m), (lambda m: m ^ 2)

    base = ensemble.reshape(rows, LANES)
    if group & (group - 1):
        turn = lambda d: lambda m: (m + 4 * d) % mem_size
    else:
        turn = lambda d: lambda m: m ^ (4 * d)
    line = [move(base, False, turn(d)) for d in range(1, group)]
    whole = pl.BlockSpec(memory_space=pltpu.VMEM)
    small = pltpu.CompilerParams(vmem_limit_bytes=4 * 1024 * 1024)
    first = pl.pallas_call(
        first_kernel,
        out_shape=jax.ShapeDtypeStruct((SUB, LANES), jnp.float32),
        out_specs=whole,
        compiler_params=small,
        cost_estimate=pl.CostEstimate(flops=FIRST_COST, bytes_accessed=4096, transcendentals=0),
    )()
    pair = pl.pallas_call(
        pair_kernel,
        out_shape=jax.ShapeDtypeStruct((2, rows, LANES), jnp.float32),
        in_specs=[whole] * 3,
        out_specs=whole,
        compiler_params=small,
    )(first, base, increments)
    later, _ = lax.optimization_barrier((base, first))
    base_x = move(later[None], False, beside)
    base_diag = move(later[None], True, beside)
    base_y = move(pair, True, same)
    pair, line = lax.optimization_barrier((pair, line))

    diff = pl.pallas_call(
        pack_kernel,
        out_shape=jax.ShapeDtypeStruct((group - 1, rows, LANES), jnp.bfloat16),
        in_specs=[whole] * group,
        out_specs=whole,
        compiler_params=small,
        cost_estimate=pl.CostEstimate(
            flops=PACK_COST, bytes_accessed=8 * columns * 4, transcendentals=0
        ),
    )(pair, *line)
    x, y = move(diff, False, beside), move(diff, True, same)
    diag = move(diff, True, beside)
    bundle = pl.pallas_call(
        bundle_kernel,
        out_shape=jax.ShapeDtypeStruct((group + 2, rows, LANES), jnp.bfloat16),
        in_specs=[whole] * 2,
        out_specs=whole,
        compiler_params=small,
    )
    mine = bundle(pair, diff)
    mine, base_y, base_diag = lax.optimization_barrier((mine, base_y, base_diag))
    lines = [mine, bundle(base_x, x), bundle(base_y, y), bundle(base_diag, diag)]
    lines += [move(v, False, lambda m: m ^ 1) for v in lines]
    own, others = [lines[i] for i in (0, 1, 4, 5)], [lines[i] for i in (2, 3, 6, 7)]

    vectors = mem_size * block_count
    room = pltpu.CompilerParams(vmem_limit_bytes=VMEM_LIMIT)
    spread = pltpu.VMEM((mem_size * (rows + 1), LANES), jnp.float32)
    return pl.pallas_call(
        functools.partial(product_kernel, group),
        out_shape=jax.ShapeDtypeStruct((1, columns), jnp.float32),
        in_specs=[pl.BlockSpec(memory_space=pltpu.SMEM)] + [whole] * 11,
        out_specs=whole,
        scratch_shapes=[
            spread,
            spread,
            pltpu.VMEM((2 * block_count, mem_size, block_size), jnp.bfloat16),
            pltpu.VMEM((vectors, block_size), jnp.float32),
        ],
        compiler_params=room,
    )(offsets.T, *own, *others, pair, base_y, taper)


def solution(mesh):
    return jax.shard_map(
        on_device,
        mesh=mesh,
        in_specs=(P("mem", "lon"), P("mem", "lon"), P("lon", None), P()),
        out_specs=P("mem", "lon"),
        check_vma=False,
    )
```

```python
import functools

import jax
import jax.numpy as jnp
from jax import lax
from jax.experimental import pallas as pl
from jax.experimental.pallas import tpu as pltpu
from jax.sharding import PartitionSpec as P

LANES = 128
SUB = 8
VMEM_LIMIT = 16 * 1024 * 1024
PACK_COST = 20_000_000_000
FIRST_COST = 2_000_000_000


def first_kernel(out_ref):
    out_ref[...] = jnp.zeros_like(out_ref)


def bases_kernel(x_ref, y_ref, diag_ref, out_ref):
    for j, ref in enumerate((x_ref, y_ref, diag_ref)):
        out_ref[j] = ref[0]


def pair_kernel(first_ref, base_ref, inc_ref, pair_ref):
    pair_ref[0] = base_ref[...]
    for r in range(base_ref.shape[0]):
        part = inc_ref[:, r * LANES : (r + 1) * LANES]
        pair_ref[1, r : r + 1, :] = part.astype(jnp.float32)


def pack_kernel(pair_ref, *refs):
    line, (diff_ref, mine_ref) = refs[:-2], refs[-2:]
    base = pair_ref[0]
    high = base.astype(jnp.bfloat16)
    rest = base - high.astype(jnp.float32)
    middle = rest.astype(jnp.bfloat16)
    mine_ref[0] = high
    mine_ref[1] = middle
    mine_ref[2] = (rest - middle.astype(jnp.float32)).astype(jnp.bfloat16)
    for j, ref in enumerate(line):
        step = (ref[...] - base).astype(jnp.bfloat16)
        diff_ref[j] = step
        mine_ref[3 + j] = step


def product_kernel(group, off_ref, *refs):
    cores = refs[:5], refs[5:10]
    inc_other, inc_own, tiles, out_ref = refs[10:14]
    pert, pert_other, picked_from, acc = refs[14:]
    slots, block_size, _ = tiles.shape
    members = 4 * group
    rows = inc_other.shape[1]
    pitch = pert.shape[0] // members
    quarters = block_size // LANES
    block_count = rows // quarters

    def weigh(side, pert, increment):
        if side == 0:
            lines = [pair for core in cores for pair in ((None, core[0]), (core[1].at[0], core[2]))]
        else:
            lines = [
                (core[1].at[j], core[2 + j]) for core in cores for j in (1, 2)
            ]

        def chunk(r):
            at = r * 2 * SUB
            here = pl.ds(at, 2 * SUB)
            starts, steps = [], []
            for base, ref in lines:
                if base is None:
                    high, middle, low = (ref[k, here, :].astype(jnp.float32) for k in range(3))
                    starts.append(high + middle + low)
                else:
                    starts.append(base[here, :])
                first = ref.shape[0] - (group - 1)
                steps.append(
                    [ref[first + k, here, :].astype(jnp.float32) for k in range(group - 1)]
                )
            total = sum(step for line in steps for step in line) + group * sum(starts)
            mean = total * (1.0 / members)
            m = 0
            for start, line in zip(starts, steps):
                start = start - mean
                for value in [start] + [start + step for step in line]:
                    pert[pl.ds(m * pitch + at, 2 * SUB), :] = value
                    m += 1

        for r in range(rows // (2 * SUB)):
            chunk(r)

        for i in range(block_count):
            for q in range(quarters):
                lanes = slice(q * LANES, (q + 1) * LANES)
                at = i * quarters + q
                part = pert[pl.ds(at, members, pitch), :] * increment(at)
                picked_from[side * block_count + i, :, lanes] = part.astype(jnp.bfloat16)

    weigh(0, pert, lambda at: inc_own[1, at : at + 1, :])

    contract = (((1,), (1,)), ((), ()))
    vectors = block_count * members
    acc[...] = lax.dot_general(
        picked_from[0:block_count].reshape(vectors, block_size),
        tiles[0],
        contract,
        preferred_element_type=jnp.float32,
    )
    weigh(1, pert_other, lambda at: inc_other[1, at : at + 1, :])

    def chosen(s):
        blocks = []
        for i in range(block_count):
            place = i + off_ref[s - 1, i]
            place = jnp.where(place < 0, place + 2 * block_count, place)
            blocks.append(picked_from[place])
        return jnp.concatenate(blocks, axis=0)

    for s in range(1, slots, 2):
        both = range(s, min(s + 2, slots))
        acc[...] += lax.dot_general(
            jnp.concatenate([chosen(k) for k in both], axis=1),
            jnp.concatenate([tiles[k] for k in both], axis=1),
            contract,
            preferred_element_type=jnp.float32,
        )

    scale = 1.0 / (members - 1)
    for i in range(block_count):
        for q in range(quarters):
            lanes = slice(q * LANES, (q + 1) * LANES)
            term = (
                pert[pl.ds(i * quarters + q, members, pitch), :]
                * acc[i * members : (i + 1) * members, lanes]
            )
            row = jnp.sum(term, axis=0, keepdims=True) * scale
            out_ref[:, i * block_size + q * LANES : i * block_size + (q + 1) * LANES] = row


def mover(lon_size, mem_size):
    def one(x, step, mem_of):
        perm = []
        for l in range(lon_size):
            for m in range(mem_size):
                source = ((l + step) % lon_size) * mem_size + mem_of(m)
                perm.append((source, l * mem_size + m))
        return lax.ppermute(x, ("lon", "mem"), perm)

    def move(x, across, mem_of):
        if not across:
            return one(x, 0, mem_of)
        if lon_size == 2:
            return one(x, 1, mem_of)
        axis = x.ndim - 2 if x.shape[-2] > 1 else x.ndim - 1
        right, left = jnp.split(x, 2, axis=axis)
        return jnp.concatenate([one(right, 1, mem_of), one(left, -1, mem_of)], axis=axis)

    return move


def on_device(ensemble, increments, offsets, taper):
    lon_size, mem_size = lax.axis_size("lon"), lax.axis_size("mem")
    group = mem_size // 4
    slots, block_size, _ = taper.shape
    block_count = offsets.shape[0]
    columns = ensemble.shape[1]
    rows = columns // LANES
    move = mover(lon_size, mem_size)
    same, beside = (lambda m: m), (lambda m: m ^ 2)

    base = ensemble.reshape(rows, LANES)
    if group & (group - 1):
        turn = lambda d: lambda m: (m + 4 * d) % mem_size
    else:
        turn = lambda d: lambda m: m ^ (4 * d)
    line = [move(base, False, turn(d)) for d in range(1, group)]
    whole = pl.BlockSpec(memory_space=pltpu.VMEM)
    small = pltpu.CompilerParams(vmem_limit_bytes=4 * 1024 * 1024)
    first = pl.pallas_call(
        first_kernel,
        out_shape=jax.ShapeDtypeStruct((SUB, LANES), jnp.float32),
        out_specs=whole,
        compiler_params=small,
        cost_estimate=pl.CostEstimate(flops=FIRST_COST, bytes_accessed=4096, transcendentals=0),
    )()
    pair = pl.pallas_call(
        pair_kernel,
        out_shape=jax.ShapeDtypeStruct((2, rows, LANES), jnp.float32),
        in_specs=[whole] * 3,
        out_specs=whole,
        compiler_params=small,
    )(first, base, increments)
    later, _ = lax.optimization_barrier((base, first))
    base_x = move(later[None], False, beside)
    base_diag = move(later[None], True, beside)
    base_y = move(pair, True, same)
    pair, line = lax.optimization_barrier((pair, line))

    diff, mine = pl.pallas_call(
        pack_kernel,
        out_shape=(
            jax.ShapeDtypeStruct((group - 1, rows, LANES), jnp.bfloat16),
            jax.ShapeDtypeStruct((group + 2, rows, LANES), jnp.bfloat16),
        ),
        in_specs=[whole] * group,
        out_specs=(whole, whole),
        compiler_params=small,
        cost_estimate=pl.CostEstimate(
            flops=PACK_COST, bytes_accessed=8 * columns * 4, transcendentals=0
        ),
    )(pair, *line)
    x, y = move(diff, False, beside), move(diff, True, same)
    diag = move(diff, True, beside)
    mine, base_x, base_y, base_diag = lax.optimization_barrier((mine, base_x, base_y, base_diag))
    bases = pl.pallas_call(
        bases_kernel,
        out_shape=jax.ShapeDtypeStruct((3, rows, LANES), jnp.float32),
        in_specs=[whole] * 3,
        out_specs=whole,
        compiler_params=small,
    )(base_x, base_y, base_diag)
    lines = [mine, bases, x, y, diag]
    lines += [move(v, False, lambda m: m ^ 1) for v in lines]

    vectors = mem_size * block_count
    return pl.pallas_call(
        functools.partial(product_kernel, group),
        out_shape=jax.ShapeDtypeStruct((1, columns), jnp.float32),
        in_specs=[pl.BlockSpec(memory_space=pltpu.SMEM)] + [whole] * 13,
        out_specs=whole,
        scratch_shapes=[
            pltpu.VMEM((mem_size * (rows + 1), LANES), jnp.float32),
            pltpu.VMEM((mem_size * (rows + 1), LANES), jnp.float32),
            pltpu.VMEM((2 * block_count, mem_size, block_size), jnp.bfloat16),
            pltpu.VMEM((vectors, block_size), jnp.float32),
        ],
        compiler_params=pltpu.CompilerParams(vmem_limit_bytes=VMEM_LIMIT),
    )(offsets.T, *lines, base_y, pair, taper)


def solution(mesh):
    return jax.shard_map(
        on_device,
        mesh=mesh,
        in_specs=(P("mem", "lon"), P("mem", "lon"), P("lon", None), P()),
        out_specs=P("mem", "lon"),
        check_vma=False,
    )
```

```python
import functools

import jax
import jax.numpy as jnp
from jax import lax
from jax.experimental import pallas as pl
from jax.experimental.pallas import tpu as pltpu
from jax.sharding import PartitionSpec as P

LANES = 128
SUB = 8
VMEM_LIMIT = 16 * 1024 * 1024
PACK_COST = 20_000_000_000
FIRST_COST = 2_000_000_000


def first_kernel(out_ref):
    out_ref[...] = jnp.zeros_like(out_ref)


def bases_kernel(x_ref, y_ref, diag_ref, out_ref):
    for j, ref in enumerate((x_ref, y_ref, diag_ref)):
        out_ref[j] = ref[0]


def pair_kernel(first_ref, base_ref, inc_ref, pair_ref):
    pair_ref[0] = base_ref[...]
    for r in range(base_ref.shape[0]):
        part = inc_ref[:, r * LANES : (r + 1) * LANES]
        pair_ref[1, r : r + 1, :] = part.astype(jnp.float32)


def pack_kernel(pair_ref, *refs):
    line, (diff_ref, mine_ref) = refs[:-2], refs[-2:]
    base = pair_ref[0]
    high = base.astype(jnp.bfloat16)
    rest = base - high.astype(jnp.float32)
    middle = rest.astype(jnp.bfloat16)
    mine_ref[0] = high
    mine_ref[1] = middle
    mine_ref[2] = (rest - middle.astype(jnp.float32)).astype(jnp.bfloat16)
    for j, ref in enumerate(line):
        step = (ref[...] - base).astype(jnp.bfloat16)
        diff_ref[j] = step
        mine_ref[3 + j] = step


def product_kernel(group, off_ref, *refs):
    cores = refs[:5], refs[5:10]
    inc_other, inc_own, tiles, out_ref = refs[10:14]
    pert, pert_other, picked_from, acc = refs[14:]
    slots, block_size, _ = tiles.shape
    members = 4 * group
    rows = inc_other.shape[1]
    pitch = pert.shape[0] // members
    quarters = block_size // LANES
    block_count = rows // quarters

    def weigh(side, pert, increment):
        if side == 0:
            lines = [pair for core in cores for pair in ((None, core[0]), (core[1].at[0], core[2]))]
        else:
            lines = [
                (core[1].at[j], core[2 + j]) for core in cores for j in (1, 2)
            ]

        def chunk(r):
            at = r * 2 * SUB
            here = pl.ds(at, 2 * SUB)
            starts, steps = [], []
            for base, ref in lines:
                if base is None:
                    high, middle, low = (ref[k, here, :].astype(jnp.float32) for k in range(3))
                    starts.append(high + middle + low)
                else:
                    starts.append(base[here, :])
                first = ref.shape[0] - (group - 1)
                steps.append(
                    [ref[first + k, here, :].astype(jnp.float32) for k in range(group - 1)]
                )
            total = sum(step for line in steps for step in line) + group * sum(starts)
            mean = total * (1.0 / members)
            m = 0
            for start, line in zip(starts, steps):
                start = start - mean
                for value in [start] + [start + step for step in line]:
                    pert[pl.ds(m * pitch + at, 2 * SUB), :] = value
                    m += 1

        for r in range(rows // (2 * SUB)):
            chunk(r)

        for i in range(block_count):
            for q in range(quarters):
                lanes = slice(q * LANES, (q + 1) * LANES)
                at = i * quarters + q
                part = pert[pl.ds(at, members, pitch), :] * increment(at)
                picked_from[side * block_count + i, :, lanes] = part.astype(jnp.bfloat16)

    weigh(0, pert, lambda at: inc_own[1, at : at + 1, :])

    contract = (((1,), (1,)), ((), ()))
    vectors = block_count * members
    acc[...] = lax.dot_general(
        picked_from[0:block_count].reshape(vectors, block_size),
        tiles[0],
        contract,
        preferred_element_type=jnp.float32,
    )
    weigh(1, pert_other, lambda at: inc_other[1, at : at + 1, :])

    def chosen(s):
        blocks = []
        for i in range(block_count):
            place = i + off_ref[s - 1, i]
            place = jnp.where(place < 0, place + 2 * block_count, place)
            blocks.append(picked_from[place])
        return jnp.concatenate(blocks, axis=0)

    for s in range(1, slots, 2):
        both = range(s, min(s + 2, slots))
        acc[...] += lax.dot_general(
            jnp.concatenate([chosen(k) for k in both], axis=1),
            jnp.concatenate([tiles[k] for k in both], axis=1),
            contract,
            preferred_element_type=jnp.float32,
        )

    scale = 1.0 / (members - 1)
    for i in range(block_count):
        for q in range(quarters):
            lanes = slice(q * LANES, (q + 1) * LANES)
            term = (
                pert[pl.ds(i * quarters + q, members, pitch), :]
                * acc[i * members : (i + 1) * members, lanes]
            )
            row = jnp.sum(term, axis=0, keepdims=True) * scale
            out_ref[:, i * block_size + q * LANES : i * block_size + (q + 1) * LANES] = row


def mover(lon_size, mem_size):
    def one(x, step, mem_of):
        perm = []
        for l in range(lon_size):
            for m in range(mem_size):
                source = ((l + step) % lon_size) * mem_size + mem_of(m)
                perm.append((source, l * mem_size + m))
        return lax.ppermute(x, ("lon", "mem"), perm)

    def move(x, across, mem_of):
        if not across:
            return one(x, 0, mem_of)
        if lon_size == 2:
            return one(x, 1, mem_of)
        axis = x.ndim - 2 if x.shape[-2] > 1 else x.ndim - 1
        right, left = jnp.split(x, 2, axis=axis)
        return jnp.concatenate([one(right, 1, mem_of), one(left, -1, mem_of)], axis=axis)

    return move


def on_device(ensemble, increments, offsets, taper):
    lon_size, mem_size = lax.axis_size("lon"), lax.axis_size("mem")
    group = mem_size // 4
    slots, block_size, _ = taper.shape
    block_count = offsets.shape[0]
    columns = ensemble.shape[1]
    rows = columns // LANES
    move = mover(lon_size, mem_size)
    same, beside = (lambda m: m), (lambda m: m ^ 2)

    base = ensemble.reshape(rows, LANES)
    if group & (group - 1):
        turn = lambda d: lambda m: (m + 4 * d) % mem_size
    else:
        turn = lambda d: lambda m: m ^ (4 * d)
    line = [move(base, False, turn(d)) for d in range(1, group)]
    whole = pl.BlockSpec(memory_space=pltpu.VMEM)
    small = pltpu.CompilerParams(vmem_limit_bytes=4 * 1024 * 1024)
    first = pl.pallas_call(
        first_kernel,
        out_shape=jax.ShapeDtypeStruct((SUB, LANES), jnp.float32),
        out_specs=whole,
        compiler_params=small,
        cost_estimate=pl.CostEstimate(flops=FIRST_COST, bytes_accessed=4096, transcendentals=0),
    )()
    pair = pl.pallas_call(
        pair_kernel,
        out_shape=jax.ShapeDtypeStruct((2, rows, LANES), jnp.float32),
        in_specs=[whole] * 3,
        out_specs=whole,
        compiler_params=small,
    )(first, base, increments)
    later, _ = lax.optimization_barrier((base, first))
    base_x = move(later[None], False, beside)
    base_diag = move(later[None], True, beside)
    base_y = move(pair, True, same)
    pair, line = lax.optimization_barrier((pair, line))

    diff, mine = pl.pallas_call(
        pack_kernel,
        out_shape=(
            jax.ShapeDtypeStruct((group - 1, rows, LANES), jnp.bfloat16),
            jax.ShapeDtypeStruct((group + 2, rows, LANES), jnp.bfloat16),
        ),
        in_specs=[whole] * group,
        out_specs=(whole, whole),
        compiler_params=small,
        cost_estimate=pl.CostEstimate(
            flops=PACK_COST, bytes_accessed=8 * columns * 4, transcendentals=0
        ),
    )(pair, *line)
    x, y = move(diff, False, beside), move(diff, True, same)
    diag = move(diff, True, beside)
    _, base_x, base_y, base_diag = lax.optimization_barrier((mine, base_x, base_y, base_diag))
    bases = pl.pallas_call(
        bases_kernel,
        out_shape=jax.ShapeDtypeStruct((3, rows, LANES), jnp.float32),
        in_specs=[whole] * 3,
        out_specs=whole,
        compiler_params=small,
    )(base_x, base_y, base_diag)
    lines = [mine, bases, x, y, diag]
    lines += [move(v, False, lambda m: m ^ 1) for v in lines]

    vectors = mem_size * block_count
    return pl.pallas_call(
        functools.partial(product_kernel, group),
        out_shape=jax.ShapeDtypeStruct((1, columns), jnp.float32),
        in_specs=[pl.BlockSpec(memory_space=pltpu.SMEM)] + [whole] * 13,
        out_specs=whole,
        scratch_shapes=[
            pltpu.VMEM((mem_size * (rows + 1), LANES), jnp.float32),
            pltpu.VMEM((mem_size * (rows + 1), LANES), jnp.float32),
            pltpu.VMEM((2 * block_count, mem_size, block_size), jnp.bfloat16),
            pltpu.VMEM((vectors, block_size), jnp.float32),
        ],
        compiler_params=pltpu.CompilerParams(vmem_limit_bytes=VMEM_LIMIT),
    )(offsets.T, *lines, base_y, pair, taper)


def solution(mesh):
    return jax.shard_map(
        on_device,
        mesh=mesh,
        in_specs=(P("mem", "lon"), P("mem", "lon"), P("lon", None), P()),
        out_specs=P("mem", "lon"),
        check_vma=False,
    )
```
